256 devices in a mesh: grp: 16 (over x_hi, y, core), loc: 16 (over z, x_lo).
Axes of the slice: x: 4 (x_hi: 2, x_lo: 2; x = x_hi * 2 + x_lo), y: 4, z: 8, core: 2. Of those that a mesh axis runs over, the one named last changes fastest.
Arguments:
- queries: bfloat16 [65536, 2048], P(('grp', 'loc')), may hold values from -5 to 5
- keys: bfloat16 [65536, 2048], P(('grp', 'loc')), may hold values from -5 to 5
- values: bfloat16 [65536, 2048], P(('grp', 'loc')), may hold values from -6 to 6
- grad_out: bfloat16 [65536, 2048], P(('grp', 'loc')), may hold values from -48 to 48
Outputs:
- attended: bfloat16 [65536, 2048], P(('grp', 'loc'))
- grad_queries: bfloat16 [65536, 2048], P(('grp', 'loc'))
- grad_keys: bfloat16 [65536, 2048], P(('grp', 'loc'))
- grad_values: bfloat16 [65536, 2048], P(('grp', 'loc'))
The draws below stay inside these ranges and needn't reach their ends.
All inputs are finite; a program needn't handle non-finite values.
Results may differ from the reference program's by a relative error of at most 0.02.
Values may be sent and summed in bfloat16 or wider, within the bound.
No kernel may reach another device: no remote copies, remote signals or barrier semaphores. Data moves between devices by JAX's collectives and lax.ppermute only.
A program may use at most 192 MiB of HBM per device.

```python
import math
import jax
import jax.numpy as jnp
from jax import lax

HEADS = 16
HDIM = 128
BLK = 128
P2 = 64
P3 = 256
GROUP_TOK = 4096
TOKENS = 65536


def draw_queries(key, part):
    key = jax.random.fold_in(key, 11)
    feat_width = HEADS * HDIM
    base_draw = jax.random.truncated_normal(key, -4.0, 4.0, (TOKENS, feat_width)).astype(jnp.float32)
    return base_draw.astype(jnp.bfloat16)


def draw_keys(key, part):
    key = jax.random.fold_in(key, 23)
    feat_width = HEADS * HDIM
    base_draw = jax.random.truncated_normal(key, -4.0, 4.0, (TOKENS, feat_width)).astype(jnp.float32)
    return base_draw.astype(jnp.bfloat16)


def level_of(own_key, extent, split, low, high):
    level, own = 1.0, jax.random.fold_in(own_key, 6)
    for axis_at, shards_of in split:
        steps = jnp.exp(jax.random.uniform(jax.random.fold_in(own, axis_at), (shards_of,), jnp.float32, low / len(split), high / len(split)))
        level = level * jnp.repeat(steps, extent[axis_at] // shards_of).reshape([-1 if axis == axis_at else 1 for axis in range(len(extent))])
    return level


def scatter_about(stream_key, extent, width, most, split=(), kind=jnp.bfloat16):
    values = jax.random.normal(stream_key, extent, jnp.float32) * width
    if len(split) > 0:
        values = level_of(stream_key, extent, split, -0.22, 0.18) * values
    return jnp.clip(values, min=-most, max=most).astype(kind)


def setup_inputs(seed: int = 0) -> dict:
    seeds = jax.random.split(jax.random.key(seed), 5)
    queries = draw_queries(jax.random.fold_in(seeds[4], 71), 0)
    keys = draw_keys(jax.random.fold_in(seeds[4], 71), 0)
    values = scatter_about(seeds[2], (TOKENS, HEADS * HDIM), 1.0, 6.0, ((0, 256),))
    grad_out = scatter_about(seeds[3], (TOKENS, HEADS * HDIM), 8.0, 48.0, ((0, 256),))
    return {"queries": queries, "keys": keys, "values": values, "grad_out": grad_out}


NEG_BIG = -1e+30

def settle(tensor):
    return lax.optimization_barrier(tensor.astype(jnp.bfloat16)).astype(jnp.float32)

def pool_runs(tokens_in, run_len, factor):
    dims_in = tokens_in.shape
    grouped = tokens_in.reshape(dims_in[:-2] + (dims_in[-2] // run_len, run_len, dims_in[-1])).astype(jnp.float32)
    return (lax.optimization_barrier(jnp.sum(grouped, axis=-2)) / factor).astype(jnp.bfloat16)

def block_terms(query_blk, key_set, value_set, allowed, grad_blk):
    row_count = query_blk.shape[0]
    key_count = key_set.shape[0]
    feat_width = HEADS * HDIM
    score_scale = 1.0 / math.sqrt(HDIM)
    query_h = query_blk.reshape(row_count, HEADS, HDIM).astype(jnp.float32)
    key_h = key_set.reshape(key_count, HEADS, HDIM).astype(jnp.float32)
    value_h = value_set.reshape(key_count, HEADS, HDIM).astype(jnp.float32)
    grad_h = grad_blk.reshape(row_count, HEADS, HDIM).astype(jnp.float32)
    scores = jnp.einsum('qhd,khd->hqk', query_h, key_h) * score_scale
    scores = jnp.where(allowed[None, :, :], scores, NEG_BIG)
    summit = lax.optimization_barrier(jnp.max(scores, axis=2, keepdims=True))
    expo_terms = jnp.exp(scores - summit)
    totals = lax.optimization_barrier(jnp.sum(expo_terms, axis=2, keepdims=True))
    mixed_sum = jnp.einsum('hqk,khd->qhd', settle(expo_terms), value_h)
    attended = (mixed_sum / jnp.transpose(totals, (1, 0, 2))).astype(jnp.bfloat16)
    deltas = lax.optimization_barrier(jnp.sum(grad_h * attended.astype(jnp.float32), axis=2))
    weights = expo_terms / totals
    grad_value = jnp.einsum('hqk,qhd->khd', settle(weights), grad_h)
    dot_grad = jnp.einsum('qhd,khd->hqk', grad_h, value_h)
    dscore = settle(weights * (dot_grad - jnp.transpose(deltas)[:, :, None]) * score_scale)
    grad_query = jnp.einsum('hqk,khd->qhd', dscore, key_h).astype(jnp.bfloat16)
    grad_key = jnp.einsum('hqk,qhd->khd', dscore, query_h)
    return (attended.reshape(row_count, feat_width), grad_query.reshape(row_count, feat_width), grad_key.reshape(key_count, feat_width), grad_value.reshape(key_count, feat_width))

def reference(queries, keys, values, grad_out):
    feat_width = HEADS * HDIM
    per_group = GROUP_TOK // P2
    third_count = TOKENS // P3
    level_two_k = pool_runs(keys, P2, math.sqrt(P2))
    level_two_v = pool_runs(values, P2, math.sqrt(P2))
    level_three_k = pool_runs(level_two_k, 4, 2.0)
    level_three_v = pool_runs(level_two_v, 4, 2.0)
    third_group = jnp.arange(third_count, dtype=jnp.int32) * P3 // GROUP_TOK
    zero_rows = jnp.zeros((BLK, feat_width), jnp.bfloat16)
    padded_k = jnp.concatenate([zero_rows, keys], axis=0)
    padded_v = jnp.concatenate([zero_rows, values], axis=0)
    fine_off = jnp.arange(2 * BLK, dtype=jnp.int32)
    query_off = jnp.arange(BLK, dtype=jnp.int32)
    entry_end = (jnp.arange(per_group, dtype=jnp.int32) + 1) * P2
    two_edge = 2 * BLK + per_group

    def scan_step(state_in, block_idx):
        hold_k, hold_v, acc_two_k, acc_two_v, acc_three_k, acc_three_v = state_in
        blk_start = block_idx * BLK
        group_idx = blk_start // GROUP_TOK
        query_blk = lax.dynamic_slice_in_dim(queries, blk_start, BLK, 0)
        grad_blk = lax.dynamic_slice_in_dim(grad_out, blk_start, BLK, 0)
        win_k = lax.dynamic_slice_in_dim(padded_k, blk_start, 2 * BLK, 0)
        win_v = lax.dynamic_slice_in_dim(padded_v, blk_start, 2 * BLK, 0)
        sec_start = (group_idx * per_group).astype(jnp.int32)
        sec_k = lax.dynamic_slice_in_dim(level_two_k, sec_start, per_group, 0)
        sec_v = lax.dynamic_slice_in_dim(level_two_v, sec_start, per_group, 0)
        key_set = jnp.concatenate([win_k, sec_k, level_three_k], axis=0)
        value_set = jnp.concatenate([win_v, sec_v, level_three_v], axis=0)
        query_pos = blk_start + query_off
        key_pos = blk_start - BLK + fine_off
        fine_ok = (key_pos[None, :] <= query_pos[:, None]) & (key_pos[None, :] >= 0)
        second_ok = group_idx * GROUP_TOK + entry_end <= blk_start - BLK
        third_ok = third_group < group_idx
        allowed = jnp.concatenate([fine_ok, jnp.broadcast_to(second_ok[None, :], (BLK, per_group)), jnp.broadcast_to(third_ok[None, :], (BLK, third_count))], axis=1)
        attended, grad_query, grad_key, grad_value = block_terms(query_blk, key_set, value_set, allowed, grad_blk)
        done_k = hold_k + grad_key[:BLK]
        done_v = hold_v + grad_value[:BLK]
        old_k = lax.dynamic_slice_in_dim(acc_two_k, sec_start, per_group, 0)
        old_v = lax.dynamic_slice_in_dim(acc_two_v, sec_start, per_group, 0)
        acc_two_k = lax.dynamic_update_slice_in_dim(acc_two_k, old_k + grad_key[2 * BLK:two_edge], sec_start, 0)
        acc_two_v = lax.dynamic_update_slice_in_dim(acc_two_v, old_v + grad_value[2 * BLK:two_edge], sec_start, 0)
        acc_three_k = acc_three_k + grad_key[two_edge:]
        acc_three_v = acc_three_v + grad_value[two_edge:]
        state_out = (grad_key[BLK:2 * BLK], grad_value[BLK:2 * BLK], acc_two_k, acc_two_v, acc_three_k, acc_three_v)
        return (state_out, (attended, grad_query, done_k, done_v))
    start_state = (jnp.zeros((BLK, feat_width), jnp.float32), jnp.zeros((BLK, feat_width), jnp.float32), jnp.zeros((TOKENS // P2, feat_width), jnp.float32), jnp.zeros((TOKENS // P2, feat_width), jnp.float32), jnp.zeros((third_count, feat_width), jnp.float32), jnp.zeros((third_count, feat_width), jnp.float32))
    final_state, stacked = lax.scan(scan_step, start_state, jnp.arange(TOKENS // BLK, dtype=jnp.int32))
    hold_k, hold_v, acc_two_k, acc_two_v, acc_three_k, acc_three_v = final_state
    attended_all, grad_q_all, done_k, done_v = stacked
    fine_k = jnp.concatenate([done_k[1:].reshape(-1, feat_width), hold_k], axis=0)
    fine_v = jnp.concatenate([done_v[1:].reshape(-1, feat_width), hold_v], axis=0)
    total_two_k = acc_two_k + jnp.repeat(acc_three_k / 2.0, 4, axis=0)
    total_two_v = acc_two_v + jnp.repeat(acc_three_v / 2.0, 4, axis=0)
    grad_keys = (fine_k + jnp.repeat(total_two_k / math.sqrt(P2), P2, axis=0)).astype(jnp.bfloat16)
    grad_values = (fine_v + jnp.repeat(total_two_v / math.sqrt(P2), P2, axis=0)).astype(jnp.bfloat16)
    return (attended_all.reshape(TOKENS, feat_width), grad_q_all.reshape(TOKENS, feat_width), grad_keys, grad_values)
```

```python
import math

import jax
import jax.numpy as jnp
import numpy as np
from jax import lax
from jax.experimental import pallas as pl
from jax.experimental.pallas import tpu as pltpu
from jax.sharding import Mesh, PartitionSpec as P

HEADS = 16
HDIM = 128
BLK = 128
P2 = 64
FEAT = HEADS * HDIM
NEG_BIG = -1e30
LOG2E = math.log2(math.e)
SCALE = 1.0 / math.sqrt(HDIM)

NXH, NY, NC, NZ, NXL = 2, 4, 2, 8, 2
AXES = ("xh", "y", "c", "z", "xl")
N2 = NZ * NXL * 4
N3G = NZ * NXL
N3 = N3G * NXH * NY * NC
NP = N2 + N3
HPB = 4


def nt(a, b):
    return lax.dot_general(a, b, (((1,), (1,)), ((), ())), preferred_element_type=jnp.float32)


def nn(a, b):
    return lax.dot_general(a, b, (((1,), (0,)), ((), ())), preferred_element_type=jnp.float32)


def tn(a, b):
    return lax.dot_general(a, b, (((0,), (0,)), ((), ())), preferred_element_type=jnp.float32)


def one_head(bias_ref, seg, refs, outs):
    q_ref, k_ref, v_ref, g_ref, prior_x_ref, prior_z_ref, pk2_ref, pv2_ref = refs[:8]
    thirds = refs[8:]
    att_ref, dq_ref, dk_ref, dv_ref, dprior_ref, g2_ref, near_ref, far_ref = outs
    q = q_ref[:, seg]
    k = k_ref[:, seg]
    v = v_ref[:, seg]
    g = g_ref[:, seg]
    prior_k = prior_x_ref[0, :, seg] + prior_z_ref[0, :, seg]
    prior_v = prior_x_ref[1, :, seg] + prior_z_ref[1, :, seg]
    pk = jnp.concatenate(
        [pk2_ref[:, seg]] + [t[s, 0, :, seg] for t in thirds for s in range(NXH)], axis=0
    )
    pv = jnp.concatenate(
        [pv2_ref[:, seg]] + [t[s, 1, :, seg] for t in thirds for s in range(NXH)], axis=0
    )
    c2 = SCALE * LOG2E
    key_i = lax.broadcasted_iota(jnp.int32, (BLK, BLK), 0)
    qry_i = lax.broadcasted_iota(jnp.int32, (BLK, BLK), 1)
    causal = key_i <= qry_i
    q0, q1 = q[:BLK], q[BLK:]
    g0, g1 = g[:BLK], g[BLK:]
    k0, k1 = k[:BLK], k[BLK:]
    v0, v1 = v[:BLK], v[BLK:]

    sp = nt(pk, q) * c2 + bias_ref[BLK:, :]
    s_prior = nt(prior_k, q0) * c2 + bias_ref[:BLK, :BLK]
    s_k0 = nt(k0, q) * c2
    s00 = jnp.where(causal, s_k0[:, :BLK], NEG_BIG)
    s01 = s_k0[:, BLK:]
    s11 = jnp.where(causal, nt(k1, q1) * c2, NEG_BIG)

    fine = ((s_prior, s00), (s01, s11))
    fine_k = ((prior_v, v0), (v0, v1))
    expo, invs, atts, deltas = [], [], [], []
    for b in range(2):
        cols = slice(b * BLK, (b + 1) * BLK)
        sa, sb = fine[b]
        spb = sp[:, cols]
        top = jnp.maximum(
            jnp.max(spb, axis=0, keepdims=True), jnp.max(jnp.maximum(sa, sb), axis=0, keepdims=True)
        )
        ea = jnp.exp2(sa - top)
        eb = jnp.exp2(sb - top)
        ep = jnp.exp2(spb - top)
        tot = jnp.sum(ea + eb, axis=0, keepdims=True) + jnp.sum(ep, axis=0, keepdims=True)
        inv = 1.0 / tot
        invs.append(inv)
        expo.append((ea, eb, ep))
    ep_all = jnp.concatenate(
        [expo[0][2].astype(jnp.bfloat16), expo[1][2].astype(jnp.bfloat16)], axis=1
    )
    mixed_p = tn(ep_all, pv)
    g32 = g.astype(jnp.float32)
    for b in range(2):
        rows = slice(b * BLK, (b + 1) * BLK)
        va, vb = fine_k[b]
        ea, eb, _ = expo[b]
        mixed = mixed_p[rows] + tn(ea.astype(jnp.bfloat16), va) + tn(eb.astype(jnp.bfloat16), vb)
        inv_col = jnp.transpose(jnp.broadcast_to(invs[b], (8, BLK)))[:, 0:1]
        att = (mixed * inv_col).astype(jnp.bfloat16)
        att_ref[rows, seg] = att
        delta_col = jnp.sum(g32[rows] * att.astype(jnp.float32), axis=1, keepdims=True)
        deltas.append(jnp.transpose(jnp.broadcast_to(delta_col, (BLK, BLK)))[0:1, :])

    dp = nt(pv, g)
    d_prior = nt(prior_v, g0)
    d_k0 = nt(v0, g)
    d11 = nt(v1, g1)
    dots = ((d_prior, d_k0[:, :BLK]), (d_k0[:, BLK:], d11))
    ws, ds = [], []
    for b in range(2):
        cols = slice(b * BLK, (b + 1) * BLK)
        wts = [e * invs[b] for e in expo[b]]
        dot_b = dots[b] + (dp[:, cols],)
        ws.append([w.astype(jnp.bfloat16) for w in wts])
        ds.append(
            [(w * SCALE * (d - deltas[b])).astype(jnp.bfloat16) for w, d in zip(wts, dot_b)]
        )
    wp = jnp.concatenate([ws[0][2], ws[1][2]], axis=1)
    dsp = jnp.concatenate([ds[0][2], ds[1][2]], axis=1)
    wk0 = jnp.concatenate([ws[0][1], ws[1][0]], axis=1)
    dsk0 = jnp.concatenate([ds[0][1], ds[1][0]], axis=1)

    dq = tn(dsp, pk)
    dq0 = dq[:BLK] + tn(ds[0][0], prior_k) + tn(ds[0][1], k0)
    dq1 = dq[BLK:] + tn(ds[1][0], k0) + tn(ds[1][1], k1)
    dq_ref[:BLK, seg] = dq0.astype(jnp.bfloat16)
    dq_ref[BLK:, seg] = dq1.astype(jnp.bfloat16)

    dprior_ref[0, :, seg] = nn(ds[0][0], q0).astype(jnp.bfloat16)
    dprior_ref[1, :, seg] = nn(ws[0][0], g0).astype(jnp.bfloat16)
    dk_ref[:BLK, seg] = nn(dsk0, q)
    dk_ref[BLK:, seg] = nn(ds[1][1], q1)
    dv_ref[:BLK, seg] = nn(wk0, g)
    dv_ref[BLK:, seg] = nn(ws[1][1], g1)
    gkp = nn(dsp, q)
    gvp = nn(wp, g)
    for kv, part in enumerate((gkp, gvp)):
        for s in range(NZ):
            g2_ref[s, kv, :, seg] = part[s * 8 : s * 8 + 8]
        for s in range(2 * NY * NXH):
            lo = N2 + s * N3G
            ref = near_ref if s < NY * NXH else far_ref
            ref[s // NXH % NY, s % NXH, kv, :, seg] = part[lo : lo + N3G].astype(jnp.bfloat16)


def attn_kernel(bias_ref, *refs):
    for h in range(HPB):
        seg = slice(h * HDIM, (h + 1) * HDIM)
        one_head(bias_ref, seg, refs[:16], refs[16:])


def cols(width, *lead):
    zeros = (0,) * len(lead)
    return pl.BlockSpec(lead + (width,), lambda i: zeros + (i,))


def attention(bias, q, k, v, g, prior_x, prior_z, pk2, pv2, thirds):
    width = HPB * HDIM
    rows = q.shape[0]
    shape = jax.ShapeDtypeStruct
    row_spec = cols(width, rows)
    sums_spec = cols(width, NY, NXH, 2, N3G)
    return pl.pallas_call(
        attn_kernel,
        grid=(FEAT // width,),
        in_specs=[
            pl.BlockSpec((BLK + NP, 2 * BLK), lambda i: (0, 0)),
            row_spec, row_spec, row_spec, row_spec,
            cols(width, 2, BLK), cols(width, 2, BLK), cols(width, N2), cols(width, N2),
        ] + [cols(width, NXH, 2, N3G)] * 8,
        out_specs=[
            row_spec, row_spec, row_spec, row_spec,
            cols(width, 2, BLK), cols(width, NZ, 2, 8), sums_spec, sums_spec,
        ],
        out_shape=[
            shape((rows, FEAT), jnp.bfloat16),
            shape((rows, FEAT), jnp.bfloat16),
            shape((rows, FEAT), jnp.float32),
            shape((rows, FEAT), jnp.float32),
            shape((2, BLK, FEAT), jnp.bfloat16),
            shape((NZ, 2, 8, FEAT), jnp.float32),
            shape((NY, NXH, 2, N3G, FEAT), jnp.bfloat16),
            shape((NY, NXH, 2, N3G, FEAT), jnp.bfloat16),
        ],
        compiler_params=pltpu.CompilerParams(vmem_limit_bytes=48 * 1024 * 1024),
        cost_estimate=pl.CostEstimate(
            flops=6 * 2 * 2 * BLK * 576 * FEAT, bytes_accessed=20 << 20, transcendentals=0
        ),
    )(bias, q, k, v, g, prior_x, prior_z, pk2, pv2, *thirds)


def pool_kernel(k_ref, v_ref, pooled_ref, last_ref):
    for kv, ref in ((0, k_ref), (1, v_ref)):
        last_ref[kv] = ref[BLK:, :]
        for e in range(4):
            run = ref[e * P2 : (e + 1) * P2, :].astype(jnp.float32)
            total = jnp.sum(run, axis=0, keepdims=True) * (1.0 / math.sqrt(P2))
            pooled_ref[kv, e : e + 1, :] = total.astype(jnp.bfloat16)


def pool(k, v):
    width = 512
    rows = k.shape[0]
    shape = jax.ShapeDtypeStruct
    return pl.pallas_call(
        pool_kernel,
        grid=(FEAT // width,),
        in_specs=[cols(width, rows)] * 2,
        out_specs=[cols(width, 2, 4), cols(width, 2, BLK)],
        out_shape=[
            shape((2, 4, FEAT), jnp.bfloat16),
            shape((2, BLK, FEAT), jnp.bfloat16),
        ],
        compiler_params=pltpu.CompilerParams(vmem_limit_bytes=32 * 1024 * 1024),
        cost_estimate=pl.CostEstimate(flops=1 << 20, bytes_accessed=3 << 20, transcendentals=0),
    )(k, v)


def gathered_kernel(*refs):
    pieces, (pk_ref, pv_ref, third_ref) = refs[:NZ], refs[NZ:]
    for kv, out in ((0, pk_ref), (1, pv_ref)):
        parts = [p[kv].astype(jnp.float32) for p in pieces]
        out[...] = jnp.concatenate(parts, axis=0).astype(jnp.bfloat16)
        sums = [
            jnp.sum(p[lo : lo + 4], axis=0, keepdims=True) * 0.5 for p in parts for lo in (0, 4)
        ]
        third_ref[0, kv] = jnp.concatenate(sums, axis=0).astype(jnp.bfloat16)


def gathered(pieces):
    width = 1024
    shape = jax.ShapeDtypeStruct
    return pl.pallas_call(
        gathered_kernel,
        grid=(FEAT // width,),
        in_specs=[cols(width, 2, 8)] * NZ,
        out_specs=[cols(width, N2), cols(width, N2), cols(width, 1, 2, N3G)],
        out_shape=[
            shape((N2, FEAT), jnp.bfloat16),
            shape((N2, FEAT), jnp.bfloat16),
            shape((NXH, 2, N3G, FEAT), jnp.bfloat16),
        ],
        compiler_params=pltpu.CompilerParams(vmem_limit_bytes=32 * 1024 * 1024),
        cost_estimate=pl.CostEstimate(flops=1 << 20, bytes_accessed=1 << 20, transcendentals=0),
    )(*pieces)


def lifted_kernel(g2_ref, mine_ref, other_ref, *outs):
    for kv in range(2):
        third = (mine_ref[kv] + other_ref[kv].astype(jnp.float32)) * 0.5
        for s in range(NZ):
            lift = jnp.concatenate(
                [jnp.broadcast_to(third[s * 2 + i : s * 2 + i + 1], (4, third.shape[1])) for i in range(2)],
                axis=0,
            )
            outs[s][kv] = (g2_ref[s, kv] + lift).astype(outs[s].dtype)


def lifted(g2, mine, other):
    width = 1024
    shape = jax.ShapeDtypeStruct
    return pl.pallas_call(
        lifted_kernel,
        grid=(FEAT // width,),
        in_specs=[cols(width, NZ, 2, 8), cols(width, 2, N3G), cols(width, 2, N3G)],
        out_specs=[cols(width, 2, 8)] * NZ,
        out_shape=[
            shape((2, 8, FEAT), jnp.float32 if s == 0 else jnp.bfloat16) for s in range(NZ)
        ],
        compiler_params=pltpu.CompilerParams(vmem_limit_bytes=32 * 1024 * 1024),
        cost_estimate=pl.CostEstimate(flops=1 << 20, bytes_accessed=2 << 20, transcendentals=0),
    )(g2, mine, other)


def finish_kernel(dk_ref, dv_ref, back_x_ref, back_z_ref, two_ref, gk_ref, gv_ref):
    for kv, src, dst in ((0, dk_ref, gk_ref), (1, dv_ref, gv_ref)):
        for part in range(4):
            lo = part * P2
            spread = two_ref[kv, part : part + 1, :]
            val = src[lo : lo + P2, :] + spread
            if part >= 2:
                rows = slice(lo - BLK, lo - BLK + P2)
                back = back_x_ref[kv, rows, :] + back_z_ref[kv, rows, :]
                val = val + back.astype(jnp.float32)
            dst[lo : lo + P2, :] = val.astype(jnp.bfloat16)


def finish(dk, dv, back_x, back_z, two):
    rows = dk.shape[0]
    width = 512
    shape = jax.ShapeDtypeStruct
    return pl.pallas_call(
        finish_kernel,
        grid=(FEAT // width,),
        in_specs=[cols(width, rows)] * 2 + [cols(width, 2, BLK)] * 2 + [cols(width, 2, 4)],
        out_specs=[cols(width, rows)] * 2,
        out_shape=[shape((rows, FEAT), jnp.bfloat16)] * 2,
        compiler_params=pltpu.CompilerParams(vmem_limit_bytes=48 * 1024 * 1024),
        cost_estimate=pl.CostEstimate(flops=1 << 20, bytes_accessed=7 << 20, transcendentals=0),
    )(dk, dv, back_x, back_z, two)


def ring(value, axis, size, step):
    return lax.ppermute(value, axis, [(i, (i + step) % size) for i in range(size)])


def bf(x):
    return x.astype(jnp.bfloat16)


def f32(x):
    return x.astype(jnp.float32)


def per_device(queries, keys, values, grad_out):
    xh, y, c, z, xl = (lax.axis_index(a) for a in AXES)
    group = xh * (NY * NC) + y * NC + c
    shard = z * NXL + xl
    count = NXH * NY * NC * NZ * NXL

    pooled, last = pool(keys, values)
    pair = jnp.concatenate([pooled, ring(pooled, "xl", NXL, 1)], axis=1)
    last, pair = lax.optimization_barrier((last, pair))
    prior_x = lax.ppermute(last, AXES, [(i, i + 1) for i in range(0, count - 1, 2)])
    pieces = [pair] + [ring(pair, "z", NZ, s) for s in range(1, NZ)]
    pk2, pv2, third = gathered(pieces)
    own_third = third[0]
    prior_x, last, own_third = lax.optimization_barrier((prior_x, last, own_third))
    prior_z = lax.ppermute(last, AXES, [(i, i + 1) for i in range(1, count - 1, 2)])
    third = third.at[1].set(ring(own_third, "xh", NXH, 1))
    thirds = [third] + [ring(third, "y", NY, s) for s in range(1, NY)]
    thirds = thirds + [ring(t, "c", NC, 1) for t in thirds]

    r2 = jnp.arange(N2, dtype=jnp.int32)
    from_shard = ((z - r2 // 8) % NZ) * NXL + (xl + r2 // 4) % NXL
    entry = from_shard * 4 + r2 % 4
    ok2 = entry[:, None] < (4 * shard - 2 + 2 * jnp.arange(2, dtype=jnp.int32))[None, :]
    r3 = jnp.arange(N3, dtype=jnp.int32)
    per_xh, per_y = N3G, N3G * NXH
    per_c = per_y * NY
    from_group = (
        ((xh + r3 // per_xh) % NXH) * (NY * NC)
        + ((y - (r3 // per_y) % NY) % NY) * NC
        + (c + r3 // per_c) % NC
    )
    ok3 = jnp.broadcast_to((from_group < group)[:, None], (N3, 2))
    ok_prior = jnp.broadcast_to((group * (NZ * NXL) + shard) > 0, (BLK, 2))
    allowed = jnp.concatenate([ok_prior, ok2, ok3], axis=0)
    bias = jnp.repeat(jnp.where(allowed, 0.0, NEG_BIG).astype(jnp.float32), BLK, axis=1)

    attended, grad_q, dk, dv, dprior, g2, near, far = attention(
        bias, queries, keys, values, grad_out, prior_x, prior_z, pk2, pv2, thirds
    )

    back_z = lax.ppermute(dprior, AXES, [(i + 1, i) for i in range(1, count - 1, 2)])

    far = ring(far, "c", NC, 1)
    s3 = [f32(near[s]) + f32(far[s]) for s in range(NY)]
    t3 = s3[0]
    for s in range(1, NY):
        t3 = t3 + f32(ring(bf(s3[s]), "y", NY, -s))
    other = ring(bf(t3[1]), "xh", NXH, 1)
    dprior, other = lax.optimization_barrier((dprior, other))
    back_x = lax.ppermute(dprior, AXES, [(i + 1, i) for i in range(0, count - 1, 2)])
    parts = lifted(g2, t3[0], other)
    two = parts[0]
    for s in range(1, NZ):
        two = two + f32(ring(parts[s], "z", NZ, -s))
    back_z, two = lax.optimization_barrier((back_z, two))
    two = two[:, :4] + f32(ring(bf(two[:, 4:]), "xl", NXL, 1))
    two = two / math.sqrt(P2)
    grad_k, grad_v = finish(dk, dv, back_x, back_z, two)
    return attended, grad_q, grad_k, grad_v


def solution(mesh):
    fine_mesh = Mesh(np.asarray(mesh.devices).reshape(NXH, NY, NC, NZ, NXL), AXES)
    spec = P(AXES, None)
    return jax.shard_map(
        per_device,
        mesh=fine_mesh,
        in_specs=(spec,) * 4,
        out_specs=(spec,) * 4,
        check_vma=False,
    )
```

```python
import math

import jax
import jax.numpy as jnp
import numpy as np
from jax import lax
from jax.experimental import pallas as pl
from jax.experimental.pallas import tpu as pltpu
from jax.sharding import Mesh, PartitionSpec as P

HEADS = 16
HDIM = 128
BLK = 128
P2 = 64
FEAT = HEADS * HDIM
NEG_BIG = -1e30
LOG2E = math.log2(math.e)
SCALE = 1.0 / math.sqrt(HDIM)

NXH, NY, NC, NZ, NXL = 2, 4, 2, 8, 2
AXES = ("xh", "y", "c", "z", "xl")
N2 = NZ * NXL * 4
N3G = NZ * NXL
N3 = N3G * NXH * NY * NC
NP = N2 + N3
HPB = 4
Z_ORDER = (4, 5, 3, 6, 2, 7, 1)
Y_STEP = (0, 1, 3, 2)


def nt(a, b):
    return lax.dot_general(a, b, (((1,), (1,)), ((), ())), preferred_element_type=jnp.float32)


def nn(a, b):
    return lax.dot_general(a, b, (((1,), (0,)), ((), ())), preferred_element_type=jnp.float32)


def tn(a, b):
    return lax.dot_general(a, b, (((0,), (0,)), ((), ())), preferred_element_type=jnp.float32)


def one_head(odd, bias_ref, seg, refs, outs):
    q_ref, k_ref, v_ref, g_ref, across_ref, along_ref, pk2_ref, pv2_ref = refs[:8]
    thirds = refs[8:]
    att_ref, dq_ref, dk_ref, dv_ref, dprior_ref, g2_ref, near_ref, far_ref = outs
    q = q_ref[:, seg]
    k = k_ref[:, seg]
    v = v_ref[:, seg]
    g = g_ref[:, seg]
    prior_k = jnp.where(odd, across_ref[0, :, seg], along_ref[0, :, seg])
    prior_v = jnp.where(odd, across_ref[1, :, seg], along_ref[1, :, seg])
    pk = jnp.concatenate(
        [pk2_ref[:, seg]] + [t[s, 0, :, seg] for t in thirds for s in range(NXH)], axis=0
    )
    pv = jnp.concatenate(
        [pv2_ref[:, seg]] + [t[s, 1, :, seg] for t in thirds for s in range(NXH)], axis=0
    )
    c2 = SCALE * LOG2E
    key_i = lax.broadcasted_iota(jnp.int32, (BLK, BLK), 0)
    qry_i = lax.broadcasted_iota(jnp.int32, (BLK, BLK), 1)
    causal = key_i <= qry_i
    q0, q1 = q[:BLK], q[BLK:]
    g0, g1 = g[:BLK], g[BLK:]
    k0, k1 = k[:BLK], k[BLK:]
    v0, v1 = v[:BLK], v[BLK:]

    sp = nt(pk, q) * c2 + bias_ref[BLK:, :]
    s_prior = nt(prior_k, q0) * c2 + bias_ref[:BLK, :BLK]
    s_k0 = nt(k0, q) * c2
    s00 = jnp.where(causal, s_k0[:, :BLK], NEG_BIG)
    s01 = s_k0[:, BLK:]
    s11 = jnp.where(causal, nt(k1, q1) * c2, NEG_BIG)

    fine = ((s_prior, s00), (s01, s11))
    fine_k = ((prior_v, v0), (v0, v1))
    expo, invs, atts, deltas = [], [], [], []
    for b in range(2):
        cols = slice(b * BLK, (b + 1) * BLK)
        sa, sb = fine[b]
        spb = sp[:, cols]
        top = jnp.maximum(
            jnp.max(spb, axis=0, keepdims=True), jnp.max(jnp.maximum(sa, sb), axis=0, keepdims=True)
        )
        ea = jnp.exp2(sa - top)
        eb = jnp.exp2(sb - top)
        ep = jnp.exp2(spb - top)
        tot = jnp.sum(ea + eb, axis=0, keepdims=True) + jnp.sum(ep, axis=0, keepdims=True)
        inv = 1.0 / tot
        invs.append(inv)
        expo.append((ea, eb, ep))
    ea_all = [e[0].astype(jnp.bfloat16) for e in expo]
    eb_all = [e[1].astype(jnp.bfloat16) for e in expo]
    ep_all = jnp.concatenate([e[2].astype(jnp.bfloat16) for e in expo], axis=1)
    mixed = tn(pv, ep_all) + tn(v0, jnp.concatenate([eb_all[0], ea_all[1]], axis=1))
    edge = jnp.concatenate([tn(prior_v, ea_all[0]), tn(v1, eb_all[1])], axis=1)
    inv_all = jnp.concatenate(invs, axis=1)
    att_t = ((mixed + edge) * inv_all).astype(jnp.bfloat16)
    att_ref[:, seg] = jnp.transpose(att_t)
    g_t = jnp.transpose(g).astype(jnp.float32)
    delta_all = jnp.sum(g_t * att_t.astype(jnp.float32), axis=0, keepdims=True)
    deltas = [delta_all[:, :BLK], delta_all[:, BLK:]]

    dp = nt(pv, g)
    d_prior = nt(prior_v, g0)
    d_k0 = nt(v0, g)
    d11 = nt(v1, g1)
    dots = ((d_prior, d_k0[:, :BLK]), (d_k0[:, BLK:], d11))
    ws, ds = [], []
    for b in range(2):
        cols = slice(b * BLK, (b + 1) * BLK)
        wts = [e * invs[b] for e in expo[b]]
        dot_b = dots[b] + (dp[:, cols],)
        ws.append([w.astype(jnp.bfloat16) for w in wts])
        ds.append(
            [(w * SCALE * (d - deltas[b])).astype(jnp.bfloat16) for w, d in zip(wts, dot_b)]
        )
    wp = jnp.concatenate([ws[0][2], ws[1][2]], axis=1)
    dsp = jnp.concatenate([ds[0][2], ds[1][2]], axis=1)
    wk0 = jnp.concatenate([ws[0][1], ws[1][0]], axis=1)
    dsk0 = jnp.concatenate([ds[0][1], ds[1][0]], axis=1)

    dq_t = tn(pk, dsp) + tn(k0, dsk0)
    dq_t = dq_t + jnp.concatenate([tn(prior_k, ds[0][0]), tn(k1, ds[1][1])], axis=1)
    dq_ref[:, seg] = jnp.transpose(dq_t.astype(jnp.bfloat16))

    dprior_ref[0, :, seg] = nn(ds[0][0], q0).astype(jnp.bfloat16)
    dprior_ref[1, :, seg] = nn(ws[0][0], g0).astype(jnp.bfloat16)
    dk_ref[:BLK, seg] = nn(dsk0, q)
    dk_ref[BLK:, seg] = nn(ds[1][1], q1)
    dv_ref[:BLK, seg] = nn(wk0, g)
    dv_ref[BLK:, seg] = nn(ws[1][1], g1)
    gkp = nn(dsp, q)
    gvp = nn(wp, g)
    for kv, part in enumerate((gkp, gvp)):
        for s in range(NZ):
            g2_ref[s, kv, :, seg] = part[s * 8 : s * 8 + 8]
        for s in range(2 * NY * NXH):
            lo = N2 + s * N3G
            ref = near_ref if s < NY * NXH else far_ref
            ref[s // NXH % NY, s % NXH, kv, :, seg] = part[lo : lo + N3G].astype(jnp.bfloat16)


def fill_bias(place_ref, bias_ref):
    xh, y, c, z, xl = (place_ref[i] for i in range(5))
    group = xh * (NY * NC) + y * NC + c
    shard = z * NXL + xl
    first = (group * (NZ * NXL) + shard) == 0
    bias_ref[:BLK, :] = jnp.full((BLK, 2 * BLK), jnp.where(first, NEG_BIG, 0.0), jnp.float32)
    r2 = lax.broadcasted_iota(jnp.int32, (N2, 2 * BLK), 0)
    late = lax.broadcasted_iota(jnp.int32, (N2, 2 * BLK), 1) // BLK
    from_shard = ((z + NZ - r2 // 8) % NZ) * NXL + (xl + r2 // 4) % NXL
    ok2 = from_shard * 4 + r2 % 4 < 4 * shard - 2 + 2 * late
    bias_ref[BLK : BLK + N2, :] = jnp.where(ok2, 0.0, NEG_BIG)
    for s in range(2 * NY * NXH):
        of_xh = (xh + s % NXH) % NXH
        of_y = (y + NY - Y_STEP[s // NXH % NY]) % NY
        of_c = (c + s // (NXH * NY)) % NC
        ok3 = of_xh * (NY * NC) + of_y * NC + of_c < group
        lo = BLK + N2 + s * N3G
        bias_ref[lo : lo + N3G, :] = jnp.full(
            (N3G, 2 * BLK), jnp.where(ok3, 0.0, NEG_BIG), jnp.float32
        )


def attn_kernel(place_ref, *refs):
    bias_ref = refs[-1]

    @pl.when(pl.program_id(0) == 0)
    def _():
        fill_bias(place_ref, bias_ref)

    odd = place_ref[4] == 1
    for h in range(HPB):
        seg = slice(h * HDIM, (h + 1) * HDIM)
        one_head(odd, bias_ref, seg, refs[:16], refs[16:24])


def cols(width, *lead):
    zeros = (0,) * len(lead)
    return pl.BlockSpec(lead + (width,), lambda i: zeros + (i,))


def attention(place, q, k, v, g, across, along, pk2, pv2, thirds):
    width = HPB * HDIM
    rows = q.shape[0]
    shape = jax.ShapeDtypeStruct
    row_spec = cols(width, rows)
    sums_spec = cols(width, NY, NXH, 2, N3G)
    return pl.pallas_call(
        attn_kernel,
        grid=(FEAT // width,),
        in_specs=[
            pl.BlockSpec(memory_space=pltpu.SMEM),
            row_spec, row_spec, row_spec, row_spec,
            cols(width, 2, BLK), cols(width, 2, BLK), cols(width, N2), cols(width, N2),
        ] + [cols(width, NXH, 2, N3G)] * 8,
        out_specs=[
            row_spec, row_spec, row_spec, row_spec,
            cols(width, 2, BLK), cols(width, NZ, 2, 8), sums_spec, sums_spec,
        ],
        out_shape=[
            shape((rows, FEAT), jnp.bfloat16),
            shape((rows, FEAT), jnp.bfloat16),
            shape((rows, FEAT), jnp.float32),
            shape((rows, FEAT), jnp.float32),
            shape((2, BLK, FEAT), jnp.bfloat16),
            shape((NZ, 2, 8, FEAT), jnp.float32),
            shape((NY, NXH, 2, N3G, FEAT), jnp.bfloat16),
            shape((NY, NXH, 2, N3G, FEAT), jnp.bfloat16),
        ],
        scratch_shapes=[pltpu.VMEM((BLK + NP, 2 * BLK), jnp.float32)],
        compiler_params=pltpu.CompilerParams(vmem_limit_bytes=24 * 1024 * 1024),
        cost_estimate=pl.CostEstimate(
            flops=6 * 2 * 2 * BLK * 576 * FEAT, bytes_accessed=20 << 20, transcendentals=0
        ),
    )(place, q, k, v, g, across, along, pk2, pv2, *thirds)


def pool_kernel(k_ref, v_ref, pooled_ref):
    for kv, ref in ((0, k_ref), (1, v_ref)):
        for e in range(4):
            run = ref[e * P2 : (e + 1) * P2, :].astype(jnp.float32)
            total = jnp.sum(run, axis=0, keepdims=True) * (1.0 / math.sqrt(P2))
            pooled_ref[kv, e : e + 1, :] = total.astype(jnp.bfloat16)


def pool(k, v):
    width = 512
    return pl.pallas_call(
        pool_kernel,
        grid=(FEAT // width,),
        in_specs=[cols(width, k.shape[0])] * 2,
        out_specs=cols(width, 2, 4),
        out_shape=jax.ShapeDtypeStruct((2, 4, FEAT), jnp.bfloat16),
        compiler_params=pltpu.CompilerParams(vmem_limit_bytes=56 * 1024 * 1024),
        cost_estimate=pl.CostEstimate(flops=1 << 20, bytes_accessed=2 << 20, transcendentals=0),
    )(k, v)


def gathered_kernel(*refs):
    by_step = dict(zip((0,) + Z_ORDER[::-1], refs[:NZ]))
    pieces, (pk_ref, pv_ref, third_ref) = [by_step[s] for s in range(NZ)], refs[NZ:]
    for kv, out in ((0, pk_ref), (1, pv_ref)):
        parts = [p[kv].astype(jnp.float32) for p in pieces]
        out[...] = jnp.concatenate(parts, axis=0).astype(jnp.bfloat16)
        sums = [
            jnp.sum(p[lo : lo + 4], axis=0, keepdims=True) * 0.5 for p in parts for lo in (0, 4)
        ]
        third_ref[0, kv] = jnp.concatenate(sums, axis=0).astype(jnp.bfloat16)


def gathered(pieces):
    width = 1024
    shape = jax.ShapeDtypeStruct
    return pl.pallas_call(
        gathered_kernel,
        grid=(FEAT // width,),
        in_specs=[cols(width, 2, 8)] * NZ,
        out_specs=[cols(width, N2), cols(width, N2), cols(width, 1, 2, N3G)],
        out_shape=[
            shape((N2, FEAT), jnp.bfloat16),
            shape((N2, FEAT), jnp.bfloat16),
            shape((NXH, 2, N3G, FEAT), jnp.bfloat16),
        ],
        compiler_params=pltpu.CompilerParams(vmem_limit_bytes=32 * 1024 * 1024),
        cost_estimate=pl.CostEstimate(flops=1 << 20, bytes_accessed=1 << 20, transcendentals=0),
    )(*pieces)


def lifted_kernel(g2_ref, third_ref, *outs):
    for kv in range(2):
        for s in range(NZ):
            for i in range(NXL):
                row = slice(s * NXL + i, s * NXL + i + 1)
                lift = third_ref[0, kv, row, :] * 0.5
                part = g2_ref[s, kv, i * 4 : i * 4 + 4, :] + lift
                outs[s][kv * NXL + i] = part.astype(outs[s].dtype)
                rest = third_ref[1, kv, row, :]
                outs[s][4, kv * NXL + i : kv * NXL + i + 1, :] = rest.astype(outs[s].dtype)


def lifted(g2, third):
    width = 1024
    shape = jax.ShapeDtypeStruct
    return pl.pallas_call(
        lifted_kernel,
        grid=(FEAT // width,),
        in_specs=[cols(width, NZ, 2, 8), cols(width, NXH, 2, N3G)],
        out_specs=[cols(width, 5, 4)] * NZ,
        out_shape=[
            shape((5, 4, FEAT), jnp.float32 if s == 0 else jnp.bfloat16) for s in range(NZ)
        ],
        compiler_params=pltpu.CompilerParams(vmem_limit_bytes=24 * 1024 * 1024),
        cost_estimate=pl.CostEstimate(flops=1 << 20, bytes_accessed=2 << 20, transcendentals=0),
    )(g2, third)


def finish_kernel(dk_ref, dv_ref, back_ref, two_ref, gk_ref, gv_ref):
    for kv, src, dst in ((0, dk_ref, gk_ref), (1, dv_ref, gv_ref)):
        for part in range(4):
            lo = part * P2
            spread = two_ref[kv, part : part + 1, :]
            val = src[lo : lo + P2, :] + spread
            if part >= 2:
                rows = slice(lo - BLK, lo - BLK + P2)
                val = val + back_ref[kv, rows, :].astype(jnp.float32)
            dst[lo : lo + P2, :] = val.astype(jnp.bfloat16)


def finish(dk, dv, back, two):
    rows = dk.shape[0]
    width = 512
    shape = jax.ShapeDtypeStruct
    return pl.pallas_call(
        finish_kernel,
        grid=(FEAT // width,),
        in_specs=[cols(width, rows)] * 2 + [cols(width, 2, BLK), cols(width, 2, 4)],
        out_specs=[cols(width, rows)] * 2,
        out_shape=[shape((rows, FEAT), jnp.bfloat16)] * 2,
        compiler_params=pltpu.CompilerParams(vmem_limit_bytes=48 * 1024 * 1024),
        cost_estimate=pl.CostEstimate(flops=1 << 20, bytes_accessed=7 << 20, transcendentals=0),
    )(dk, dv, back, two)


def in_hbm(*values):
    return [pltpu.with_memory_space_constraint(v, pltpu.HBM) for v in values]


def ring(value, axis, size, step):
    return lax.ppermute(value, axis, [(i, (i + step) % size) for i in range(size)])


def bf(x):
    return x.astype(jnp.bfloat16)


def f32(x):
    return x.astype(jnp.float32)


def across_pairs(step=1):
    groups, shards = NXH * NY * NC, NZ * NXL
    pairs = []
    for g in range(groups):
        for shard in range(shards):
            even = shard % 2 == 0
            crosses = shard == (shards - 1 if step > 0 else shards - 2)
            to = g + step if crosses else g
            if 0 <= to < groups:
                pairs.append((g * shards + shard, to * shards + shard + (1 if even else -1)))
    return pairs


def along_pairs(step):
    groups, shards = NXH * NY * NC, NZ * NXL
    return [
        (g * shards + shard, g * shards + (shard + 2 * step) % shards)
        for g in range(groups)
        for shard in range(0, shards, 2)
    ]


def per_device(queries, keys, values, grad_out):
    xh, y, c, z, xl = (lax.axis_index(a) for a in AXES)

    pooled = pool(keys, values)
    last = jnp.stack([keys[BLK:], values[BLK:]])
    pair = jnp.concatenate([pooled, ring(pooled, "xl", NXL, 1)], axis=1)
    last, pair = lax.optimization_barrier((last, pair))
    across = lax.ppermute(last, AXES, across_pairs(1))
    pieces = [pair] + [ring(pair, "z", NZ, s) for s in Z_ORDER[::-1]]
    pk2, pv2, third = gathered(pieces)
    own_third = third[0]
    across, own_third = lax.optimization_barrier((across, own_third))
    along = lax.ppermute(across, AXES, along_pairs(1))
    third = third.at[1].set(ring(own_third, "xh", NXH, 1))
    thirds = [third] + [ring(third, "y", NY, s) for s in Y_STEP[1:]]
    thirds = thirds + [ring(t, "c", NC, 1) for t in thirds]

    place = jnp.stack([xh, y, c, z, xl]).astype(jnp.int32)

    attended, grad_q, dk, dv, dprior, g2, near, far = attention(
        place, *in_hbm(queries, keys, values, grad_out, across, along, pk2, pv2), in_hbm(*thirds)
    )

    count = NXH * NY * NC * NZ * NXL
    back = lax.ppermute(dprior, AXES, [(i + 1, i) for i in range(count - 1)])

    far = ring(far, "c", NC, 1)
    s3 = [f32(near[s]) + f32(far[s]) for s in range(NY)]
    t3 = s3[0]
    for s in (3, 1, 2):
        t3 = t3 + f32(ring(bf(s3[s]), "y", NY, -Y_STEP[s]))
    parts = lifted(g2, t3)
    two = parts[0]
    for s in Z_ORDER:
        two = two + f32(ring(parts[s], "z", NZ, -s))
    back, two = lax.optimization_barrier((back, two))
    near_third = ring(bf(two[4, 0::2]), "xh", NXH, 1)
    far_third = lax.ppermute(
        bf(two[4, 1::2]), ("xh", "xl"), [(0, 3), (1, 2), (2, 1), (3, 0)]
    )
    two = two[0:4:2] + f32(ring(bf(two[1:4:2]), "xl", NXL, 1))
    two = two + 0.5 * (f32(near_third) + f32(far_third))[:, None, :]
    two = two / math.sqrt(P2)
    grad_k, grad_v = finish(dk, dv, back, two)
    return attended, grad_q, grad_k, grad_v


def solution(mesh):
    fine_mesh = Mesh(np.asarray(mesh.devices).reshape(NXH, NY, NC, NZ, NXL), AXES)
    spec = P(AXES, None)
    return jax.shard_map(
        per_device,
        mesh=fine_mesh,
        in_specs=(spec,) * 4,
        out_specs=(spec,) * 4,
        check_vma=False,
    )
```

```python
import math

import jax
import jax.numpy as jnp
import numpy as np
from jax import lax
from jax.experimental import pallas as pl
from jax.experimental.pallas import tpu as pltpu
from jax.sharding import Mesh, PartitionSpec as P

HEADS = 16
HDIM = 128
BLK = 128
P2 = 64
FEAT = HEADS * HDIM
NEG_BIG = -1e30
LOG2E = math.log2(math.e)
SCALE = 1.0 / math.sqrt(HDIM)

NXH, NY, NC, NZ, NXL = 2, 4, 2, 8, 2
AXES = ("xh", "y", "c", "z", "xl")
N2 = NZ * NXL * 4
N3G = NZ * NXL
N3 = N3G * NXH * NY * NC
NP = N2 + N3
HPB = 4
Z_ORDER = (4, 5, 3, 6, 2, 7, 1)
Y_STEP = (0, 1, 3, 2)
DIAGONAL = ((0, 3), (1, 2), (2, 1), (3, 0))


def nt(a, b):
    return lax.dot_general(a, b, (((1,), (1,)), ((), ())), preferred_element_type=jnp.float32)


def nn(a, b):
    return lax.dot_general(a, b, (((1,), (0,)), ((), ())), preferred_element_type=jnp.float32)


def tn(a, b):
    return lax.dot_general(a, b, (((0,), (0,)), ((), ())), preferred_element_type=jnp.float32)


def one_head(bias_ref, seg, refs, outs):
    q_ref, k_ref, v_ref, g_ref, prior_ref, pk2_ref, pv2_ref = refs[:7]
    thirds = refs[7:]
    att_ref, dq_ref, dk_ref, dv_ref, dprior_ref, g2_ref, near_ref, far_ref = outs
    q = q_ref[:, seg]
    k = k_ref[:, seg]
    v = v_ref[:, seg]
    g = g_ref[:, seg]
    prior_k = prior_ref[0, :, seg]
    prior_v = prior_ref[1, :, seg]
    pk = jnp.concatenate(
        [pk2_ref[:, seg]] + [t[s, 0, :, seg] for t in thirds for s in range(NXH)], axis=0
    )
    pv = jnp.concatenate(
        [pv2_ref[:, seg]] + [t[s, 1, :, seg] for t in thirds for s in range(NXH)], axis=0
    )
    c2 = SCALE * LOG2E
    key_i = lax.broadcasted_iota(jnp.int32, (BLK, BLK), 0)
    qry_i = lax.broadcasted_iota(jnp.int32, (BLK, BLK), 1)
    causal = key_i <= qry_i
    q0, q1 = q[:BLK], q[BLK:]
    g0, g1 = g[:BLK], g[BLK:]
    k0, k1 = k[:BLK], k[BLK:]
    v0, v1 = v[:BLK], v[BLK:]

    sp = nt(pk, q) * c2 + bias_ref[BLK:, :]
    s_prior = nt(prior_k, q0) * c2 + bias_ref[:BLK, :BLK]
    s_k0 = nt(k0, q) * c2
    s00 = jnp.where(causal, s_k0[:, :BLK], NEG_BIG)
    s01 = s_k0[:, BLK:]
    s11 = jnp.where(causal, nt(k1, q1) * c2, NEG_BIG)

    fine = ((s_prior, s00), (s01, s11))
    fine_k = ((prior_v, v0), (v0, v1))
    expo, invs, atts, deltas = [], [], [], []
    for b in range(2):
        cols = slice(b * BLK, (b + 1) * BLK)
        sa, sb = fine[b]
        spb = sp[:, cols]
        top = jnp.maximum(
            jnp.max(spb, axis=0, keepdims=True), jnp.max(jnp.maximum(sa, sb), axis=0, keepdims=True)
        )
        ea = jnp.exp2(sa - top)
        eb = jnp.exp2(sb - top)
        ep = jnp.exp2(spb - top)
        tot = jnp.sum(ea + eb, axis=0, keepdims=True) + jnp.sum(ep, axis=0, keepdims=True)
        inv = 1.0 / tot
        invs.append(inv)
        expo.append((ea, eb, ep))
    ea_all = [e[0].astype(jnp.bfloat16) for e in expo]
    eb_all = [e[1].astype(jnp.bfloat16) for e in expo]
    ep_all = jnp.concatenate([e[2].astype(jnp.bfloat16) for e in expo], axis=1)
    mixed = tn(pv, ep_all) + tn(v0, jnp.concatenate([eb_all[0], ea_all[1]], axis=1))
    edge = jnp.concatenate([tn(prior_v, ea_all[0]), tn(v1, eb_all[1])], axis=1)
    inv_all = jnp.concatenate(invs, axis=1)
    att_t = ((mixed + edge) * inv_all).astype(jnp.bfloat16)
    att_ref[:, seg] = jnp.transpose(att_t)
    g_t = jnp.transpose(g).astype(jnp.float32)
    delta_all = jnp.sum(g_t * att_t.astype(jnp.float32), axis=0, keepdims=True)
    deltas = [delta_all[:, :BLK], delta_all[:, BLK:]]

    dp = nt(pv, g)
    d_prior = nt(prior_v, g0)
    d_k0 = nt(v0, g)
    d11 = nt(v1, g1)
    dots = ((d_prior, d_k0[:, :BLK]), (d_k0[:, BLK:], d11))
    ws, ds = [], []
    for b in range(2):
        cols = slice(b * BLK, (b + 1) * BLK)
        wts = [e * invs[b] for e in expo[b]]
        dot_b = dots[b] + (dp[:, cols],)
        ws.append([w.astype(jnp.bfloat16) for w in wts])
        ds.append(
            [(w * SCALE * (d - deltas[b])).astype(jnp.bfloat16) for w, d in zip(wts, dot_b)]
        )
    wp = jnp.concatenate([ws[0][2], ws[1][2]], axis=1)
    dsp = jnp.concatenate([ds[0][2], ds[1][2]], axis=1)
    wk0 = jnp.concatenate([ws[0][1], ws[1][0]], axis=1)
    dsk0 = jnp.concatenate([ds[0][1], ds[1][0]], axis=1)

    dq_t = tn(pk, dsp) + tn(k0, dsk0)
    dq_t = dq_t + jnp.concatenate([tn(prior_k, ds[0][0]), tn(k1, ds[1][1])], axis=1)
    dq_ref[:, seg] = jnp.transpose(dq_t.astype(jnp.bfloat16))

    dprior_ref[0, :, seg] = nn(ds[0][0], q0).astype(jnp.bfloat16)
    dprior_ref[1, :, seg] = nn(ws[0][0], g0).astype(jnp.bfloat16)
    dk_ref[:BLK, seg] = nn(dsk0, q).astype(jnp.bfloat16)
    dk_ref[BLK:, seg] = nn(ds[1][1], q1).astype(jnp.bfloat16)
    dv_ref[:BLK, seg] = nn(wk0, g).astype(jnp.bfloat16)
    dv_ref[BLK:, seg] = nn(ws[1][1], g1).astype(jnp.bfloat16)
    gkp = nn(dsp, q)
    gvp = nn(wp, g)
    for kv, part in enumerate((gkp, gvp)):
        for s in range(NZ):
            g2_ref[s, kv, :, seg] = part[s * 8 : s * 8 + 8]
        for s in range(2 * NY * NXH):
            lo = N2 + s * N3G
            ref = near_ref if s < NY * NXH else far_ref
            ref[s // NXH % NY, s % NXH, kv, :, seg] = part[lo : lo + N3G].astype(jnp.bfloat16)


def fill_bias(place_ref, bias_ref):
    xh, y, c, z, xl = (place_ref[i] for i in range(5))
    group = xh * (NY * NC) + y * NC + c
    shard = z * NXL + xl
    first = (group * (NZ * NXL) + shard) == 0
    bias_ref[:BLK, :] = jnp.full((BLK, 2 * BLK), jnp.where(first, NEG_BIG, 0.0), jnp.float32)
    r2 = lax.broadcasted_iota(jnp.int32, (N2, 2 * BLK), 0)
    late = lax.broadcasted_iota(jnp.int32, (N2, 2 * BLK), 1) // BLK
    from_shard = ((z + NZ - r2 // 8) % NZ) * NXL + (xl + r2 // 4) % NXL
    ok2 = from_shard * 4 + r2 % 4 < 4 * shard - 2 + 2 * late
    bias_ref[BLK : BLK + N2, :] = jnp.where(ok2, 0.0, NEG_BIG)
    for s in range(2 * NY * NXH):
        of_xh = (xh + s % NXH) % NXH
        of_y = (y + NY - Y_STEP[s // NXH % NY]) % NY
        of_c = (c + s // (NXH * NY)) % NC
        ok3 = of_xh * (NY * NC) + of_y * NC + of_c < group
        lo = BLK + N2 + s * N3G
        bias_ref[lo : lo + N3G, :] = jnp.full(
            (N3G, 2 * BLK), jnp.where(ok3, 0.0, NEG_BIG), jnp.float32
        )


def attn_kernel(place_ref, *refs):
    bias_ref = refs[-1]

    @pl.when(pl.program_id(0) == 0)
    def _():
        fill_bias(place_ref, bias_ref)

    for h in range(HPB):
        seg = slice(h * HDIM, (h + 1) * HDIM)
        one_head(bias_ref, seg, refs[:15], refs[15:23])


def cols(width, *lead):
    zeros = (0,) * len(lead)
    return pl.BlockSpec(lead + (width,), lambda i: zeros + (i,))


def attention(place, q, k, v, g, prior, pk2, pv2, thirds):
    width = HPB * HDIM
    rows = q.shape[0]
    shape = jax.ShapeDtypeStruct
    row_spec = cols(width, rows)
    sums_spec = cols(width, NY, NXH, 2, N3G)
    return pl.pallas_call(
        attn_kernel,
        grid=(FEAT // width,),
        in_specs=[
            pl.BlockSpec(memory_space=pltpu.SMEM),
            row_spec, row_spec, row_spec, row_spec,
            cols(width, 2, BLK), cols(width, N2), cols(width, N2),
        ] + [cols(width, NXH, 2, N3G)] * 8,
        out_specs=[
            row_spec, row_spec, row_spec, row_spec,
            cols(width, 2, BLK), cols(width, NZ, 2, 8), sums_spec, sums_spec,
        ],
        out_shape=[
            shape((rows, FEAT), jnp.bfloat16),
            shape((rows, FEAT), jnp.bfloat16),
            shape((rows, FEAT), jnp.bfloat16),
            shape((rows, FEAT), jnp.bfloat16),
            shape((2, BLK, FEAT), jnp.bfloat16),
            shape((NZ, 2, 8, FEAT), jnp.float32),
            shape((NY, NXH, 2, N3G, FEAT), jnp.bfloat16),
            shape((NY, NXH, 2, N3G, FEAT), jnp.bfloat16),
        ],
        scratch_shapes=[pltpu.VMEM((BLK + NP, 2 * BLK), jnp.float32)],
        compiler_params=pltpu.CompilerParams(vmem_limit_bytes=24 * 1024 * 1024),
        cost_estimate=pl.CostEstimate(
            flops=6 * 2 * 2 * BLK * 576 * FEAT, bytes_accessed=20 << 20, transcendentals=0
        ),
    )(place, q, k, v, g, prior, pk2, pv2, *thirds)


def pool_kernel(k_ref, v_ref, pooled_ref, third_ref):
    for kv, ref in ((0, k_ref), (1, v_ref)):
        third = jnp.zeros((1, ref.shape[1]), jnp.float32)
        for e in range(4):
            run = ref[e * P2 : (e + 1) * P2, :].astype(jnp.float32)
            total = jnp.sum(run, axis=0, keepdims=True) * (1.0 / math.sqrt(P2))
            entry = total.astype(jnp.bfloat16)
            pooled_ref[kv, e : e + 1, :] = entry
            third = third + entry.astype(jnp.float32)
        third_ref[kv : kv + 1, :] = (third * 0.5).astype(jnp.bfloat16)


def pool(k, v):
    width = 512
    shape = jax.ShapeDtypeStruct
    return pl.pallas_call(
        pool_kernel,
        grid=(FEAT // width,),
        in_specs=[cols(width, k.shape[0])] * 2,
        out_specs=[cols(width, 2, 4), cols(width, 2)],
        out_shape=[
            shape((2, 4, FEAT), jnp.bfloat16),
            shape((2, FEAT), jnp.bfloat16),
        ],
        compiler_params=pltpu.CompilerParams(vmem_limit_bytes=24 * 1024 * 1024),
        cost_estimate=pl.CostEstimate(flops=1 << 20, bytes_accessed=2 << 20, transcendentals=0),
    )(k, v)


def joined_kernel(mine_ref, other_ref, near_ref, far_ref, out_ref):
    for kv in range(2):
        out_ref[kv * NXL] = mine_ref[kv]
        out_ref[kv * NXL + 1] = other_ref[kv]
        out_ref[4, kv * NXL : kv * NXL + 1, :] = near_ref[kv : kv + 1, :]
        out_ref[4, kv * NXL + 1 : kv * NXL + 2, :] = far_ref[kv : kv + 1, :]


def joined(mine, other, near, far):
    width = FEAT
    return pl.pallas_call(
        joined_kernel,
        grid=(1,),
        in_specs=[cols(width, 2, 4), cols(width, 2, 4), cols(width, 2), cols(width, 2)],
        out_specs=cols(width, 5, 4),
        out_shape=jax.ShapeDtypeStruct((5, 4, FEAT), jnp.bfloat16),
        compiler_params=pltpu.CompilerParams(vmem_limit_bytes=24 * 1024 * 1024),
        cost_estimate=pl.CostEstimate(flops=1 << 10, bytes_accessed=1 << 18, transcendentals=0),
    )(mine, other, near, far)


def gathered_kernel(*refs):
    by_step = dict(zip((0,) + Z_ORDER[::-1], refs[:NZ]))
    pieces, (pk_ref, pv_ref, third_ref) = [by_step[s] for s in range(NZ)], refs[NZ:]
    for kv, out in ((0, pk_ref), (1, pv_ref)):
        runs = [p[kv * NXL + i].astype(jnp.float32) for p in pieces for i in range(NXL)]
        out[...] = jnp.concatenate(runs, axis=0).astype(jnp.bfloat16)
        sums = [jnp.sum(r, axis=0, keepdims=True) * 0.5 for r in runs]
        third_ref[0, kv] = jnp.concatenate(sums, axis=0).astype(jnp.bfloat16)
        rest = [p[4, kv * NXL : kv * NXL + NXL, :].astype(jnp.float32) for p in pieces]
        third_ref[1, kv] = jnp.concatenate(rest, axis=0).astype(jnp.bfloat16)


def gathered(pieces):
    width = 1024
    shape = jax.ShapeDtypeStruct
    return pl.pallas_call(
        gathered_kernel,
        grid=(FEAT // width,),
        in_specs=[cols(width, 5, 4)] * NZ,
        out_specs=[cols(width, N2), cols(width, N2), cols(width, NXH, 2, N3G)],
        out_shape=[
            pltpu.HBM((N2, FEAT), jnp.bfloat16),
            pltpu.HBM((N2, FEAT), jnp.bfloat16),
            shape((NXH, 2, N3G, FEAT), jnp.bfloat16),
        ],
        compiler_params=pltpu.CompilerParams(vmem_limit_bytes=32 * 1024 * 1024),
        cost_estimate=pl.CostEstimate(flops=1 << 20, bytes_accessed=1 << 20, transcendentals=0),
    )(*pieces)


def lifted_kernel(g2_ref, third_ref, *outs):
    for kv in range(2):
        for s in range(NZ):
            for i in range(NXL):
                row = slice(s * NXL + i, s * NXL + i + 1)
                lift = third_ref[0, kv, row, :] * 0.5
                part = g2_ref[s, kv, i * 4 : i * 4 + 4, :] + lift
                outs[s][kv * NXL + i] = part.astype(outs[s].dtype)
                rest = third_ref[1, kv, row, :]
                outs[s][4, kv * NXL + i : kv * NXL + i + 1, :] = rest.astype(outs[s].dtype)


def lifted(g2, third):
    width = 1024
    shape = jax.ShapeDtypeStruct
    return pl.pallas_call(
        lifted_kernel,
        grid=(FEAT // width,),
        in_specs=[cols(width, NZ, 2, 8), cols(width, NXH, 2, N3G)],
        out_specs=[cols(width, 5, 4)] * NZ,
        out_shape=[
            shape((5, 4, FEAT), jnp.float32 if s == 0 else jnp.bfloat16) for s in range(NZ)
        ],
        compiler_params=pltpu.CompilerParams(vmem_limit_bytes=24 * 1024 * 1024),
        cost_estimate=pl.CostEstimate(flops=1 << 20, bytes_accessed=2 << 20, transcendentals=0),
    )(g2, third)


def finish_kernel(dk_ref, dv_ref, back_ref, two_ref, gk_ref, gv_ref):
    for kv, src, dst in ((0, dk_ref, gk_ref), (1, dv_ref, gv_ref)):
        for part in range(4):
            lo = part * P2
            spread = two_ref[kv, part : part + 1, :]
            val = src[lo : lo + P2, :].astype(jnp.float32) + spread
            if part >= 2:
                rows = slice(lo - BLK, lo - BLK + P2)
                val = val + back_ref[kv, rows, :].astype(jnp.float32)
            dst[lo : lo + P2, :] = val.astype(jnp.bfloat16)


def finish(dk, dv, back, two):
    rows = dk.shape[0]
    width = 512
    shape = jax.ShapeDtypeStruct
    return pl.pallas_call(
        finish_kernel,
        grid=(FEAT // width,),
        in_specs=[cols(width, rows)] * 2 + [cols(width, 2, BLK), cols(width, 2, 4)],
        out_specs=[cols(width, rows)] * 2,
        out_shape=[shape((rows, FEAT), jnp.bfloat16)] * 2,
        compiler_params=pltpu.CompilerParams(vmem_limit_bytes=48 * 1024 * 1024),
        cost_estimate=pl.CostEstimate(flops=1 << 20, bytes_accessed=7 << 20, transcendentals=0),
    )(dk, dv, back, two)


def in_hbm(*values):
    return [pltpu.with_memory_space_constraint(v, pltpu.HBM) for v in values]


def ring(value, axis, size, step):
    return lax.ppermute(value, axis, [(i, (i + step) % size) for i in range(size)])


def bf(x):
    return x.astype(jnp.bfloat16)


def f32(x):
    return x.astype(jnp.float32)


def per_device(queries, keys, values, grad_out):
    xh, y, c, z, xl = (lax.axis_index(a) for a in AXES)

    pooled, own = pool(keys, values)
    other = ring(pooled, "xl", NXL, 1)
    near_own = ring(own, "xh", NXH, 1)
    far_own = lax.ppermute(own, ("xh", "xl"), DIAGONAL)
    pair = joined(pooled, other, near_own, far_own)
    pieces = [pair] + [ring(pair, "z", NZ, s) for s in Z_ORDER[::-1]]
    pk2, pv2, third = gathered(pieces)
    last = jnp.stack([keys[BLK:], values[BLK:]])
    last, third = lax.optimization_barrier((last, third))
    count = NXH * NY * NC * NZ * NXL
    prior = lax.ppermute(last, AXES, [(i, i + 1) for i in range(count - 1)])
    thirds = [third] + [ring(third, "y", NY, s) for s in Y_STEP[1:]]
    thirds = thirds + [ring(t, "c", NC, 1) for t in thirds]

    place = jnp.stack([xh, y, c, z, xl]).astype(jnp.int32)

    attended, grad_q, dk, dv, dprior, g2, near, far = attention(
        place, *in_hbm(queries, keys, values, grad_out, prior, pk2, pv2), in_hbm(*thirds)
    )

    count = NXH * NY * NC * NZ * NXL
    back = lax.ppermute(dprior, AXES, [(i + 1, i) for i in range(count - 1)])

    far = ring(far, "c", NC, 1)
    s3 = [f32(near[s]) + f32(far[s]) for s in range(NY)]
    t3 = s3[0]
    for s in (3, 1, 2):
        t3 = t3 + f32(ring(bf(s3[s]), "y", NY, -Y_STEP[s]))
    back, t3 = lax.optimization_barrier((back, t3))
    parts = lifted(g2, t3)
    two = parts[0]
    for s in Z_ORDER:
        two = two + f32(ring(parts[s], "z", NZ, -s))
    near_third = ring(bf(two[4, 0::2]), "xh", NXH, 1)
    far_third = lax.ppermute(
        bf(two[4, 1::2]), ("xh", "xl"), DIAGONAL
    )
    two = two[0:4:2] + f32(ring(bf(two[1:4:2]), "xl", NXL, 1))
    two = two + 0.5 * (f32(near_third) + f32(far_third))[:, None, :]
    two = two / math.sqrt(P2)
    grad_k, grad_v = finish(dk, dv, back, two)
    return attended, grad_q, grad_k, grad_v


def solution(mesh):
    fine_mesh = Mesh(np.asarray(mesh.devices).reshape(NXH, NY, NC, NZ, NXL), AXES)
    spec = P(AXES, None)
    return jax.shard_map(
        per_device,
        mesh=fine_mesh,
        in_specs=(spec,) * 4,
        out_specs=(spec,) * 4,
        check_vma=False,
    )
```

```python
import math

import jax
import jax.numpy as jnp
import numpy as np
from jax import lax
from jax.experimental import pallas as pl
from jax.experimental.pallas import tpu as pltpu
from jax.sharding import Mesh, PartitionSpec as P

HEADS = 16
HDIM = 128
BLK = 128
P2 = 64
FEAT = HEADS * HDIM
NEG_BIG = -1e30
LOG2E = math.log2(math.e)
SCALE = 1.0 / math.sqrt(HDIM)

NXH, NY, NC, NZ, NXL = 2, 4, 2, 8, 2
AXES = ("xh", "y", "c", "z", "xl")
N2 = NZ * NXL * 4
N3G = NZ * NXL
N3 = N3G * NXH * NY * NC
NP = N2 + N3
HPB = 4
Z_ORDER = (4, 5, 3, 6, 2, 7, 1)
Y_STEP = (0, 1, 3, 2)
DIAGONAL = ((0, 3), (1, 2), (2, 1), (3, 0))


def nt(a, b):
    return lax.dot_general(a, b, (((1,), (1,)), ((), ())), preferred_element_type=jnp.float32)


def nn(a, b):
    return lax.dot_general(a, b, (((1,), (0,)), ((), ())), preferred_element_type=jnp.float32)


def tn(a, b):
    return lax.dot_general(a, b, (((0,), (0,)), ((), ())), preferred_element_type=jnp.float32)


def one_head(bias_ref, seg, refs, outs):
    q_ref, k_ref, v_ref, g_ref, prior_ref, pk2_ref, pv2_ref = refs[:7]
    thirds = refs[7:]
    att_ref, dq_ref, dk_ref, dv_ref, g2_ref, near_ref, far_ref, dprior_ref = outs
    q = q_ref[:, seg]
    k = k_ref[:, seg]
    v = v_ref[:, seg]
    g = g_ref[:, seg]
    prior_k = prior_ref[0, :, seg]
    prior_v = prior_ref[1, :, seg]
    pk = jnp.concatenate(
        [pk2_ref[:, seg]] + [t[s, 0, :, seg] for t in thirds for s in range(NXH)], axis=0
    )
    pv = jnp.concatenate(
        [pv2_ref[:, seg]] + [t[s, 1, :, seg] for t in thirds for s in range(NXH)], axis=0
    )
    c2 = SCALE * LOG2E
    key_i = lax.broadcasted_iota(jnp.int32, (BLK, BLK), 0)
    qry_i = lax.broadcasted_iota(jnp.int32, (BLK, BLK), 1)
    causal = key_i <= qry_i
    q0, q1 = q[:BLK], q[BLK:]
    g0, g1 = g[:BLK], g[BLK:]
    k0, k1 = k[:BLK], k[BLK:]
    v0, v1 = v[:BLK], v[BLK:]

    sp = nt(pk, q) * c2 + bias_ref[BLK:, :]
    s_prior = nt(prior_k, q0) * c2 + bias_ref[:BLK, :BLK]
    s_k0 = nt(k0, q) * c2
    s00 = jnp.where(causal, s_k0[:, :BLK], NEG_BIG)
    s01 = s_k0[:, BLK:]
    s11 = jnp.where(causal, nt(k1, q1) * c2, NEG_BIG)

    fine = ((s_prior, s00), (s01, s11))
    fine_k = ((prior_v, v0), (v0, v1))
    expo, invs, atts, deltas = [], [], [], []
    for b in range(2):
        cols = slice(b * BLK, (b + 1) * BLK)
        sa, sb = fine[b]
        spb = sp[:, cols]
        top = jnp.maximum(
            jnp.max(spb, axis=0, keepdims=True), jnp.max(jnp.maximum(sa, sb), axis=0, keepdims=True)
        )
        ea = jnp.exp2(sa - top)
        eb = jnp.exp2(sb - top)
        ep = jnp.exp2(spb - top)
        tot = jnp.sum(ea + eb, axis=0, keepdims=True) + jnp.sum(ep, axis=0, keepdims=True)
        inv = 1.0 / tot
        invs.append(inv)
        expo.append((ea, eb, ep))
    ea_all = [e[0].astype(jnp.bfloat16) for e in expo]
    eb_all = [e[1].astype(jnp.bfloat16) for e in expo]
    ep_all = jnp.concatenate([e[2].astype(jnp.bfloat16) for e in expo], axis=1)
    mixed = tn(pv, ep_all) + tn(v0, jnp.concatenate([eb_all[0], ea_all[1]], axis=1))
    edge = jnp.concatenate([tn(prior_v, ea_all[0]), tn(v1, eb_all[1])], axis=1)
    inv_all = jnp.concatenate(invs, axis=1)
    att_t = ((mixed + edge) * inv_all).astype(jnp.bfloat16)
    att_ref[:, seg] = jnp.transpose(att_t)
    g_t = jnp.transpose(g).astype(jnp.float32)
    delta_all = jnp.sum(g_t * att_t.astype(jnp.float32), axis=0, keepdims=True)
    deltas = [delta_all[:, :BLK], delta_all[:, BLK:]]

    dp = nt(pv, g)
    d_prior = nt(prior_v, g0)
    d_k0 = nt(v0, g)
    d11 = nt(v1, g1)
    dots = ((d_prior, d_k0[:, :BLK]), (d_k0[:, BLK:], d11))
    ws, ds = [], []
    for b in range(2):
        cols = slice(b * BLK, (b + 1) * BLK)
        wts = [e * invs[b] for e in expo[b]]
        dot_b = dots[b] + (dp[:, cols],)
        ws.append([w.astype(jnp.bfloat16) for w in wts])
        ds.append(
            [(w * SCALE * (d - deltas[b])).astype(jnp.bfloat16) for w, d in zip(wts, dot_b)]
        )
    wp = jnp.concatenate([ws[0][2], ws[1][2]], axis=1)
    dsp = jnp.concatenate([ds[0][2], ds[1][2]], axis=1)
    wk0 = jnp.concatenate([ws[0][1], ws[1][0]], axis=1)
    dsk0 = jnp.concatenate([ds[0][1], ds[1][0]], axis=1)

    dq_t = tn(pk, dsp) + tn(k0, dsk0)
    dq_t = dq_t + jnp.concatenate([tn(prior_k, ds[0][0]), tn(k1, ds[1][1])], axis=1)
    dq_ref[:, seg] = jnp.transpose(dq_t.astype(jnp.bfloat16))

    dprior_ref[0, :, seg] = nn(ds[0][0], q0).astype(jnp.bfloat16)
    dprior_ref[1, :, seg] = nn(ws[0][0], g0).astype(jnp.bfloat16)
    dk_ref[:BLK, seg] = nn(dsk0, q).astype(jnp.bfloat16)
    dk_ref[BLK:, seg] = nn(ds[1][1], q1).astype(jnp.bfloat16)
    dv_ref[:BLK, seg] = nn(wk0, g).astype(jnp.bfloat16)
    dv_ref[BLK:, seg] = nn(ws[1][1], g1).astype(jnp.bfloat16)
    gkp = nn(dsp, q)
    gvp = nn(wp, g)
    for kv, part in enumerate((gkp, gvp)):
        for s in range(NZ):
            g2_ref[s, kv, :, seg] = part[s * 8 : s * 8 + 8]
        for s in range(2 * NY * NXH):
            lo = N2 + s * N3G
            ref = near_ref if s < NY * NXH else far_ref
            ref[s // NXH % NY, s % NXH, kv, :, seg] = part[lo : lo + N3G].astype(jnp.bfloat16)


def fill_bias(place_ref, bias_ref):
    xh, y, c, z, xl = (place_ref[i] for i in range(5))
    group = xh * (NY * NC) + y * NC + c
    shard = z * NXL + xl
    first = (group * (NZ * NXL) + shard) == 0
    bias_ref[:BLK, :] = jnp.full((BLK, 2 * BLK), jnp.where(first, NEG_BIG, 0.0), jnp.float32)
    r2 = lax.broadcasted_iota(jnp.int32, (N2, 2 * BLK), 0)
    late = lax.broadcasted_iota(jnp.int32, (N2, 2 * BLK), 1) // BLK
    from_shard = ((z + NZ - r2 // 8) % NZ) * NXL + (xl + r2 // 4) % NXL
    ok2 = from_shard * 4 + r2 % 4 < 4 * shard - 2 + 2 * late
    bias_ref[BLK : BLK + N2, :] = jnp.where(ok2, 0.0, NEG_BIG)
    for s in range(2 * NY * NXH):
        of_xh = (xh + s % NXH) % NXH
        of_y = (y + NY - Y_STEP[s // NXH % NY]) % NY
        of_c = (c + s // (NXH * NY)) % NC
        ok3 = of_xh * (NY * NC) + of_y * NC + of_c < group
        lo = BLK + N2 + s * N3G
        bias_ref[lo : lo + N3G, :] = jnp.full(
            (N3G, 2 * BLK), jnp.where(ok3, 0.0, NEG_BIG), jnp.float32
        )


def attn_kernel(place_ref, *refs):
    bias_ref = refs[-1]

    @pl.when(pl.program_id(0) == 0)
    def _():
        fill_bias(place_ref, bias_ref)

    for h in range(HPB):
        seg = slice(h * HDIM, (h + 1) * HDIM)
        one_head(bias_ref, seg, refs[:15], refs[-9:-1])


def cols(width, *lead, at=0):
    zeros = (0,) * len(lead)
    return pl.BlockSpec(lead + (width,), lambda i: zeros + (i + at,))


def attention(half, place, q, k, v, g, prior, pk2, pv2, thirds, earlier):
    width = HPB * HDIM
    rows = q.shape[0]
    steps = FEAT // width // 2
    at = half * steps
    shape = jax.ShapeDtypeStruct
    row_spec = cols(width, rows, at=at)
    sums_spec = cols(width, NY, NXH, 2, N3G, at=at)
    prior_spec = cols(width, 2, BLK)
    first_alias = 8 + len(thirds)
    return pl.pallas_call(
        attn_kernel,
        grid=(steps,),
        in_specs=[
            pl.BlockSpec(memory_space=pltpu.SMEM),
            row_spec, row_spec, row_spec, row_spec,
            prior_spec, cols(width, N2, at=at), cols(width, N2, at=at),
        ]
        + [cols(width, NXH, 2, N3G, at=at)] * len(thirds)
        + [pl.BlockSpec(memory_space=pl.ANY)] * len(earlier),
        out_specs=[
            row_spec, row_spec, row_spec, row_spec,
            cols(width, NZ, 2, 8, at=at), sums_spec, sums_spec, prior_spec,
        ],
        out_shape=[
            shape((rows, FEAT), jnp.bfloat16),
            shape((rows, FEAT), jnp.bfloat16),
            shape((rows, FEAT), jnp.bfloat16),
            shape((rows, FEAT), jnp.bfloat16),
            shape((NZ, 2, 8, FEAT), jnp.float32),
            shape((NY, NXH, 2, N3G, FEAT), jnp.bfloat16),
            shape((NY, NXH, 2, N3G, FEAT), jnp.bfloat16),
            shape((2, BLK, FEAT // 2), jnp.bfloat16),
        ],
        scratch_shapes=[pltpu.VMEM((BLK + NP, 2 * BLK), jnp.float32)],
        input_output_aliases={first_alias + i: i for i in range(len(earlier))},
        compiler_params=pltpu.CompilerParams(vmem_limit_bytes=24 * 1024 * 1024),
        cost_estimate=pl.CostEstimate(
            flops=6 * 2 * BLK * 576 * FEAT, bytes_accessed=10 << 20, transcendentals=0
        ),
    )(place, q, k, v, g, prior, pk2, pv2, *thirds, *earlier)


def pool_kernel(k_ref, v_ref, pooled_ref, third_ref):
    for kv, ref in ((0, k_ref), (1, v_ref)):
        third = jnp.zeros((1, ref.shape[1]), jnp.float32)
        for e in range(4):
            run = ref[e * P2 : (e + 1) * P2, :].astype(jnp.float32)
            total = jnp.sum(run, axis=0, keepdims=True) * (1.0 / math.sqrt(P2))
            entry = total.astype(jnp.bfloat16)
            pooled_ref[kv, e : e + 1, :] = entry
            third = third + entry.astype(jnp.float32)
        third_ref[kv : kv + 1, :] = (third * 0.5).astype(jnp.bfloat16)


def pool(k, v):
    width = 512
    shape = jax.ShapeDtypeStruct
    return pl.pallas_call(
        pool_kernel,
        grid=(FEAT // width,),
        in_specs=[cols(width, k.shape[0])] * 2,
        out_specs=[cols(width, 2, 4), cols(width, 2)],
        out_shape=[
            shape((2, 4, FEAT), jnp.bfloat16),
            shape((2, FEAT), jnp.bfloat16),
        ],
        compiler_params=pltpu.CompilerParams(vmem_limit_bytes=24 * 1024 * 1024),
        cost_estimate=pl.CostEstimate(flops=1 << 20, bytes_accessed=2 << 20, transcendentals=0),
    )(k, v)


def joined_kernel(mine_ref, other_ref, near_ref, far_ref, out_ref):
    for kv in range(2):
        out_ref[kv * NXL] = mine_ref[kv]
        out_ref[kv * NXL + 1] = other_ref[kv]
        out_ref[4, kv * NXL : kv * NXL + 1, :] = near_ref[kv : kv + 1, :]
        out_ref[4, kv * NXL + 1 : kv * NXL + 2, :] = far_ref[kv : kv + 1, :]


def joined(mine, other, near, far):
    width = FEAT
    return pl.pallas_call(
        joined_kernel,
        grid=(1,),
        in_specs=[cols(width, 2, 4), cols(width, 2, 4), cols(width, 2), cols(width, 2)],
        out_specs=cols(width, 5, 4),
        out_shape=jax.ShapeDtypeStruct((5, 4, FEAT), jnp.bfloat16),
        compiler_params=pltpu.CompilerParams(vmem_limit_bytes=24 * 1024 * 1024),
        cost_estimate=pl.CostEstimate(flops=1 << 10, bytes_accessed=1 << 18, transcendentals=0),
    )(mine, other, near, far)


def gathered_kernel(*refs):
    by_step = dict(zip((0,) + Z_ORDER[::-1], refs[:NZ]))
    pieces, (pk_ref, pv_ref, third_ref) = [by_step[s] for s in range(NZ)], refs[NZ:]
    for kv, out in ((0, pk_ref), (1, pv_ref)):
        runs = [p[kv * NXL + i].astype(jnp.float32) for p in pieces for i in range(NXL)]
        out[...] = jnp.concatenate(runs, axis=0).astype(jnp.bfloat16)
        sums = [jnp.sum(r, axis=0, keepdims=True) * 0.5 for r in runs]
        third_ref[0, kv] = jnp.concatenate(sums, axis=0).astype(jnp.bfloat16)
        rest = [p[4, kv * NXL : kv * NXL + NXL, :].astype(jnp.float32) for p in pieces]
        third_ref[1, kv] = jnp.concatenate(rest, axis=0).astype(jnp.bfloat16)


def gathered(pieces):
    width = 1024
    shape = jax.ShapeDtypeStruct
    return pl.pallas_call(
        gathered_kernel,
        grid=(FEAT // width,),
        in_specs=[cols(width, 5, 4)] * NZ,
        out_specs=[cols(width, N2), cols(width, N2), cols(width, NXH, 2, N3G)],
        out_shape=[
            pltpu.HBM((N2, FEAT), jnp.bfloat16),
            pltpu.HBM((N2, FEAT), jnp.bfloat16),
            shape((NXH, 2, N3G, FEAT), jnp.bfloat16),
        ],
        compiler_params=pltpu.CompilerParams(vmem_limit_bytes=32 * 1024 * 1024),
        cost_estimate=pl.CostEstimate(flops=1 << 20, bytes_accessed=1 << 20, transcendentals=0),
    )(*pieces)


def lifted_kernel(g2_ref, third_ref, *outs):
    for kv in range(2):
        for s in range(NZ):
            for i in range(NXL):
                row = slice(s * NXL + i, s * NXL + i + 1)
                lift = third_ref[0, kv, row, :] * 0.5
                part = g2_ref[s, kv, i * 4 : i * 4 + 4, :] + lift
                outs[s][kv * NXL + i] = part.astype(outs[s].dtype)
                rest = third_ref[1, kv, row, :]
                outs[s][4, kv * NXL + i : kv * NXL + i + 1, :] = rest.astype(outs[s].dtype)


def lifted(g2, third):
    width = 1024
    shape = jax.ShapeDtypeStruct
    return pl.pallas_call(
        lifted_kernel,
        grid=(FEAT // width,),
        in_specs=[cols(width, NZ, 2, 8), cols(width, NXH, 2, N3G)],
        out_specs=[cols(width, 5, 4)] * NZ,
        out_shape=[
            shape((5, 4, FEAT), jnp.float32 if s == 0 else jnp.bfloat16) for s in range(NZ)
        ],
        compiler_params=pltpu.CompilerParams(vmem_limit_bytes=24 * 1024 * 1024),
        cost_estimate=pl.CostEstimate(flops=1 << 20, bytes_accessed=2 << 20, transcendentals=0),
    )(g2, third)


def finish_kernel(dk_ref, dv_ref, lo_ref, hi_ref, two_ref, gk_ref, gv_ref):
    low = pl.program_id(0) < pl.num_programs(0) // 2
    for kv, src, dst in ((0, dk_ref, gk_ref), (1, dv_ref, gv_ref)):
        for part in range(4):
            lo = part * P2
            spread = two_ref[kv, part : part + 1, :]
            val = src[lo : lo + P2, :].astype(jnp.float32) + spread
            if part >= 2:
                rows = slice(lo - BLK, lo - BLK + P2)
                back = jnp.where(low, lo_ref[kv, rows, :], hi_ref[kv, rows, :])
                val = val + back.astype(jnp.float32)
            dst[lo : lo + P2, :] = val.astype(jnp.bfloat16)


def finish(dk, dv, back_lo, back_hi, two):
    rows = dk.shape[0]
    width = 512
    half = FEAT // width // 2
    shape = jax.ShapeDtypeStruct
    return pl.pallas_call(
        finish_kernel,
        grid=(FEAT // width,),
        in_specs=[cols(width, rows)] * 2 + [
            pl.BlockSpec((2, BLK, width), lambda i: (0, 0, jnp.minimum(i, half - 1))),
            pl.BlockSpec((2, BLK, width), lambda i: (0, 0, jnp.maximum(i - half, 0))),
            cols(width, 2, 4),
        ],
        out_specs=[cols(width, rows)] * 2,
        out_shape=[shape((rows, FEAT), jnp.bfloat16)] * 2,
        compiler_params=pltpu.CompilerParams(vmem_limit_bytes=48 * 1024 * 1024),
        cost_estimate=pl.CostEstimate(flops=1 << 20, bytes_accessed=7 << 20, transcendentals=0),
    )(dk, dv, back_lo, back_hi, two)


def in_hbm(*values):
    return [pltpu.with_memory_space_constraint(v, pltpu.HBM) for v in values]


def ring(value, axis, size, step):
    return lax.ppermute(value, axis, [(i, (i + step) % size) for i in range(size)])


def bf(x):
    return x.astype(jnp.bfloat16)


def f32(x):
    return x.astype(jnp.float32)


def per_device(queries, keys, values, grad_out):
    xh, y, c, z, xl = (lax.axis_index(a) for a in AXES)

    pooled, own = pool(keys, values)
    other = ring(pooled, "xl", NXL, 1)
    near_own = ring(own, "xh", NXH, 1)
    far_own = lax.ppermute(own, ("xh", "xl"), DIAGONAL)
    pair = joined(pooled, other, near_own, far_own)
    pieces = [pair] + [ring(pair, "z", NZ, s) for s in Z_ORDER[::-1]]
    pk2, pv2, third = gathered(pieces)
    mid = FEAT // 2
    lasts = [
        jnp.stack([keys[BLK:, lo : lo + mid], values[BLK:, lo : lo + mid]]) for lo in (0, mid)
    ]
    *lasts, third = lax.optimization_barrier((*lasts, third))
    count = NXH * NY * NC * NZ * NXL
    priors = [lax.ppermute(x, AXES, [(i, i + 1) for i in range(count - 1)]) for x in lasts]
    thirds = [third] + [ring(third, "y", NY, s) for s in Y_STEP[1:]]
    thirds = thirds + [ring(t, "c", NC, 1) for t in thirds]

    place = jnp.stack([xh, y, c, z, xl]).astype(jnp.int32)

    fixed = in_hbm(queries, keys, values, grad_out)
    pools = (*in_hbm(pk2, pv2), in_hbm(*thirds))
    outs, backs = [], []
    for half in range(2):
        *outs, dprior = attention(half, place, *fixed, *in_hbm(priors[half]), *pools, outs)
        backs.append(lax.ppermute(dprior, AXES, [(i + 1, i) for i in range(count - 1)]))
    attended, grad_q, dk, dv, g2, near, far = outs

    backs[0], far = lax.optimization_barrier((backs[0], far))
    far = ring(far, "c", NC, 1)
    s3 = [f32(near[s]) + f32(far[s]) for s in range(NY)]
    t3 = s3[0]
    for s in (3, 1, 2):
        t3 = t3 + f32(ring(bf(s3[s]), "y", NY, -Y_STEP[s]))
    *backs, t3 = lax.optimization_barrier((*backs, t3))
    parts = lifted(g2, t3)
    two = parts[0]
    for s in Z_ORDER:
        two = two + f32(ring(parts[s], "z", NZ, -s))
    near_third = ring(bf(two[4, 0::2]), "xh", NXH, 1)
    far_third = lax.ppermute(
        bf(two[4, 1::2]), ("xh", "xl"), DIAGONAL
    )
    two = two[0:4:2] + f32(ring(bf(two[1:4:2]), "xl", NXL, 1))
    two = two + 0.5 * (f32(near_third) + f32(far_third))[:, None, :]
    two = two / math.sqrt(P2)
    grad_k, grad_v = finish(dk, dv, *backs, two)
    return attended, grad_q, grad_k, grad_v


def solution(mesh):
    fine_mesh = Mesh(np.asarray(mesh.devices).reshape(NXH, NY, NC, NZ, NXL), AXES)
    spec = P(AXES, None)
    return jax.shard_map(
        per_device,
        mesh=fine_mesh,
        in_specs=(spec,) * 4,
        out_specs=(spec,) * 4,
        check_vma=False,
    )
```

```python
import math

import jax
import jax.numpy as jnp
import numpy as np
from jax import lax
from jax.experimental import pallas as pl
from jax.experimental.pallas import tpu as pltpu
from jax.sharding import Mesh, PartitionSpec as P

HEADS = 16
HDIM = 128
BLK = 128
P2 = 64
FEAT = HEADS * HDIM
NEG_BIG = -1e30
LOG2E = math.log2(math.e)
SCALE = 1.0 / math.sqrt(HDIM)

NXH, NY, NC, NZ, NXL = 2, 4, 2, 8, 2
AXES = ("xh", "y", "c", "z", "xl")
N2 = NZ * NXL * 4
N3G = NZ * NXL
N3 = N3G * NXH * NY * NC
NP = N2 + N3
HPB = 4
Z_ORDER = (4, 5, 3, 6, 2, 7, 1)
Y_STEP = (0, 1, 3, 2)
DIAGONAL = ((0, 3), (1, 2), (2, 1), (3, 0))


def nt(a, b):
    return lax.dot_general(a, b, (((1,), (1,)), ((), ())), preferred_element_type=jnp.float32)


def nn(a, b):
    return lax.dot_general(a, b, (((1,), (0,)), ((), ())), preferred_element_type=jnp.float32)


def tn(a, b):
    return lax.dot_general(a, b, (((0,), (0,)), ((), ())), preferred_element_type=jnp.float32)


def one_head(bias_ref, seg, refs, outs):
    q_ref, k_ref, v_ref, g_ref, prior_ref, pk2_ref, pv2_ref = refs[:7]
    thirds = refs[7:]
    att_ref, dq_ref, dk_ref, dv_ref, g2_ref, near_ref, far_ref, dprior_ref = outs
    q = q_ref[:, seg]
    k = k_ref[:, seg]
    v = v_ref[:, seg]
    g = g_ref[:, seg]
    prior_k = prior_ref[0, :, seg]
    prior_v = prior_ref[1, :, seg]
    pk = jnp.concatenate(
        [pk2_ref[:, seg]] + [t[s, 0, :, seg] for t in thirds for s in range(NXH)], axis=0
    )
    pv = jnp.concatenate(
        [pv2_ref[:, seg]] + [t[s, 1, :, seg] for t in thirds for s in range(NXH)], axis=0
    )
    c2 = SCALE * LOG2E
    key_i = lax.broadcasted_iota(jnp.int32, (BLK, BLK), 0)
    qry_i = lax.broadcasted_iota(jnp.int32, (BLK, BLK), 1)
    causal = key_i <= qry_i
    q0, q1 = q[:BLK], q[BLK:]
    g0, g1 = g[:BLK], g[BLK:]
    k0, k1 = k[:BLK], k[BLK:]
    v0, v1 = v[:BLK], v[BLK:]

    sp = nt(pk, q) * c2 + bias_ref[BLK:, :]
    s_prior = nt(prior_k, q0) * c2 + bias_ref[:BLK, :BLK]
    s_k0 = nt(k0, q) * c2
    s00 = jnp.where(causal, s_k0[:, :BLK], NEG_BIG)
    s01 = s_k0[:, BLK:]
    s11 = jnp.where(causal, nt(k1, q1) * c2, NEG_BIG)

    fine = ((s_prior, s00), (s01, s11))
    fine_k = ((prior_v, v0), (v0, v1))
    expo, invs, atts, deltas = [], [], [], []
    for b in range(2):
        cols = slice(b * BLK, (b + 1) * BLK)
        sa, sb = fine[b]
        spb = sp[:, cols]
        top = jnp.maximum(
            jnp.max(spb, axis=0, keepdims=True), jnp.max(jnp.maximum(sa, sb), axis=0, keepdims=True)
        )
        ea = jnp.exp2(sa - top)
        eb = jnp.exp2(sb - top)
        ep = jnp.exp2(spb - top)
        tot = jnp.sum(ea + eb, axis=0, keepdims=True) + jnp.sum(ep, axis=0, keepdims=True)
        inv = 1.0 / tot
        invs.append(inv)
        expo.append((ea, eb, ep))
    ea_all = [e[0].astype(jnp.bfloat16) for e in expo]
    eb_all = [e[1].astype(jnp.bfloat16) for e in expo]
    ep_all = jnp.concatenate([e[2].astype(jnp.bfloat16) for e in expo], axis=1)
    mixed = tn(pv, ep_all) + tn(v0, jnp.concatenate([eb_all[0], ea_all[1]], axis=1))
    edge = jnp.concatenate([tn(prior_v, ea_all[0]), tn(v1, eb_all[1])], axis=1)
    inv_all = jnp.concatenate(invs, axis=1)
    att_t = ((mixed + edge) * inv_all).astype(jnp.bfloat16)
    att_ref[:, seg] = jnp.transpose(att_t)
    g_t = jnp.transpose(g).astype(jnp.float32)
    delta_all = jnp.sum(g_t * att_t.astype(jnp.float32), axis=0, keepdims=True)
    deltas = [delta_all[:, :BLK], delta_all[:, BLK:]]

    dp = nt(pv, g)
    d_prior = nt(prior_v, g0)
    d_k0 = nt(v0, g)
    d11 = nt(v1, g1)
    dots = ((d_prior, d_k0[:, :BLK]), (d_k0[:, BLK:], d11))
    ws, ds = [], []
    for b in range(2):
        cols = slice(b * BLK, (b + 1) * BLK)
        wts = [e * invs[b] for e in expo[b]]
        dot_b = dots[b] + (dp[:, cols],)
        ws.append([w.astype(jnp.bfloat16) for w in wts])
        ds.append(
            [(w * SCALE * (d - deltas[b])).astype(jnp.bfloat16) for w, d in zip(wts, dot_b)]
        )
    wp = jnp.concatenate([ws[0][2], ws[1][2]], axis=1)
    dsp = jnp.concatenate([ds[0][2], ds[1][2]], axis=1)
    wk0 = jnp.concatenate([ws[0][1], ws[1][0]], axis=1)
    dsk0 = jnp.concatenate([ds[0][1], ds[1][0]], axis=1)

    dq_t = tn(pk, dsp) + tn(k0, dsk0)
    dq_t = dq_t + jnp.concatenate([tn(prior_k, ds[0][0]), tn(k1, ds[1][1])], axis=1)
    dq_ref[:, seg] = jnp.transpose(dq_t.astype(jnp.bfloat16))

    dprior_ref[0, :, seg] = nn(ds[0][0], q0).astype(jnp.bfloat16)
    dprior_ref[1, :, seg] = nn(ws[0][0], g0).astype(jnp.bfloat16)
    dk_ref[:BLK, seg] = nn(dsk0, q).astype(jnp.bfloat16)
    dk_ref[BLK:, seg] = nn(ds[1][1], q1).astype(jnp.bfloat16)
    dv_ref[:BLK, seg] = nn(wk0, g).astype(jnp.bfloat16)
    dv_ref[BLK:, seg] = nn(ws[1][1], g1).astype(jnp.bfloat16)
    gkp = nn(dsp, q)
    gvp = nn(wp, g)
    for kv, part in enumerate((gkp, gvp)):
        for s in range(NZ):
            g2_ref[s, kv, :, seg] = part[s * 8 : s * 8 + 8]
        for s in range(2 * NY * NXH):
            lo = N2 + s * N3G
            ref = near_ref if s < NY * NXH else far_ref
            ref[s // NXH % NY, s % NXH, kv, :, seg] = part[lo : lo + N3G].astype(jnp.bfloat16)


def fill_bias(place_ref, bias_ref):
    xh, y, c, z, xl = (place_ref[i] for i in range(5))
    group = xh * (NY * NC) + y * NC + c
    shard = z * NXL + xl
    first = (group * (NZ * NXL) + shard) == 0
    bias_ref[:BLK, :] = jnp.full((BLK, 2 * BLK), jnp.where(first, NEG_BIG, 0.0), jnp.float32)
    r2 = lax.broadcasted_iota(jnp.int32, (N2, 2 * BLK), 0)
    late = lax.broadcasted_iota(jnp.int32, (N2, 2 * BLK), 1) // BLK
    from_shard = ((z + NZ - r2 // 8) % NZ) * NXL + (xl + r2 // 4) % NXL
    ok2 = from_shard * 4 + r2 % 4 < 4 * shard - 2 + 2 * late
    bias_ref[BLK : BLK + N2, :] = jnp.where(ok2, 0.0, NEG_BIG)
    for s in range(2 * NY * NXH):
        of_xh = (xh + s % NXH) % NXH
        of_y = (y + NY - Y_STEP[s // NXH % NY]) % NY
        of_c = (c + s // (NXH * NY)) % NC
        ok3 = of_xh * (NY * NC) + of_y * NC + of_c < group
        lo = BLK + N2 + s * N3G
        bias_ref[lo : lo + N3G, :] = jnp.full(
            (N3G, 2 * BLK), jnp.where(ok3, 0.0, NEG_BIG), jnp.float32
        )


def attn_kernel(place_ref, *refs):
    bias_ref = refs[-1]

    @pl.when(pl.program_id(0) == 0)
    def _():
        fill_bias(place_ref, bias_ref)

    for h in range(HPB):
        seg = slice(h * HDIM, (h + 1) * HDIM)
        one_head(bias_ref, seg, refs[:15], refs[-9:-1])


def cols(width, *lead, at=0):
    zeros = (0,) * len(lead)
    return pl.BlockSpec(lead + (width,), lambda i: zeros + (i + at,))


def attention(half, place, q, k, v, g, prior, pk2, pv2, thirds, earlier):
    width = HPB * HDIM
    rows = q.shape[0]
    steps = FEAT // width // 2
    at = half * steps
    shape = jax.ShapeDtypeStruct
    row_spec = cols(width, rows, at=at)
    sums_spec = cols(width, NY, NXH, 2, N3G, at=at)
    prior_spec = cols(width, 2, BLK)
    first_alias = 8 + len(thirds)
    return pl.pallas_call(
        attn_kernel,
        grid=(steps,),
        in_specs=[
            pl.BlockSpec(memory_space=pltpu.SMEM),
            row_spec, row_spec, row_spec, row_spec,
            prior_spec, cols(width, N2, at=at), cols(width, N2, at=at),
        ]
        + [cols(width, NXH, 2, N3G, at=at)] * len(thirds)
        + [pl.BlockSpec(memory_space=pl.ANY)] * len(earlier),
        out_specs=[
            row_spec, row_spec, row_spec, row_spec,
            cols(width, NZ, 2, 8, at=at), sums_spec, sums_spec, prior_spec,
        ],
        out_shape=[
            shape((rows, FEAT), jnp.bfloat16),
            shape((rows, FEAT), jnp.bfloat16),
            shape((rows, FEAT), jnp.bfloat16),
            shape((rows, FEAT), jnp.bfloat16),
            shape((NZ, 2, 8, FEAT), jnp.float32),
            shape((NY, NXH, 2, N3G, FEAT), jnp.bfloat16),
            shape((NY, NXH, 2, N3G, FEAT), jnp.bfloat16),
            shape((2, BLK, FEAT // 2), jnp.bfloat16),
        ],
        scratch_shapes=[pltpu.VMEM((BLK + NP, 2 * BLK), jnp.float32)],
        input_output_aliases={first_alias + i: i for i in range(len(earlier))},
        compiler_params=pltpu.CompilerParams(vmem_limit_bytes=24 * 1024 * 1024),
        cost_estimate=pl.CostEstimate(
            flops=6 * 2 * BLK * 576 * FEAT, bytes_accessed=10 << 20, transcendentals=0
        ),
    )(place, q, k, v, g, prior, pk2, pv2, *thirds, *earlier)


def pool_kernel(k_ref, v_ref, pooled_ref, third_ref):
    for kv, ref in ((0, k_ref), (1, v_ref)):
        third = jnp.zeros((1, ref.shape[1]), jnp.float32)
        for e in range(4):
            run = ref[e * P2 : (e + 1) * P2, :].astype(jnp.float32)
            total = jnp.sum(run, axis=0, keepdims=True) * (1.0 / math.sqrt(P2))
            entry = total.astype(jnp.bfloat16)
            pooled_ref[kv, e : e + 1, :] = entry
            third = third + entry.astype(jnp.float32)
        third_ref[kv : kv + 1, :] = (third * 0.5).astype(jnp.bfloat16)


def pool(k, v):
    width = 512
    shape = jax.ShapeDtypeStruct
    return pl.pallas_call(
        pool_kernel,
        grid=(FEAT // width,),
        in_specs=[cols(width, k.shape[0])] * 2,
        out_specs=[cols(width, 2, 4), cols(width, 2)],
        out_shape=[
            shape((2, 4, FEAT), jnp.bfloat16),
            shape((2, FEAT), jnp.bfloat16),
        ],
        compiler_params=pltpu.CompilerParams(vmem_limit_bytes=24 * 1024 * 1024),
        cost_estimate=pl.CostEstimate(flops=1 << 20, bytes_accessed=2 << 20, transcendentals=0),
    )(k, v)


def joined_kernel(mine_ref, other_ref, near_ref, far_ref, out_ref):
    for kv in range(2):
        out_ref[kv * NXL] = mine_ref[kv]
        out_ref[kv * NXL + 1] = other_ref[kv]
        out_ref[4, kv * NXL : kv * NXL + 1, :] = near_ref[kv : kv + 1, :]
        out_ref[4, kv * NXL + 1 : kv * NXL + 2, :] = far_ref[kv : kv + 1, :]


def joined(mine, other, near, far):
    width = FEAT
    return pl.pallas_call(
        joined_kernel,
        grid=(1,),
        in_specs=[cols(width, 2, 4), cols(width, 2, 4), cols(width, 2), cols(width, 2)],
        out_specs=cols(width, 5, 4),
        out_shape=jax.ShapeDtypeStruct((5, 4, FEAT), jnp.bfloat16),
        compiler_params=pltpu.CompilerParams(vmem_limit_bytes=24 * 1024 * 1024),
        cost_estimate=pl.CostEstimate(flops=1 << 10, bytes_accessed=1 << 18, transcendentals=0),
    )(mine, other, near, far)


def gathered_kernel(*refs):
    by_step = dict(zip((0,) + Z_ORDER[::-1], refs[:NZ]))
    pieces, (pk_ref, pv_ref, third_ref) = [by_step[s] for s in range(NZ)], refs[NZ:]
    for kv, out in ((0, pk_ref), (1, pv_ref)):
        runs = [p[kv * NXL + i].astype(jnp.float32) for p in pieces for i in range(NXL)]
        out[...] = jnp.concatenate(runs, axis=0).astype(jnp.bfloat16)
        sums = [jnp.sum(r, axis=0, keepdims=True) * 0.5 for r in runs]
        third_ref[0, kv] = jnp.concatenate(sums, axis=0).astype(jnp.bfloat16)
        rest = [p[4, kv * NXL : kv * NXL + NXL, :].astype(jnp.float32) for p in pieces]
        third_ref[1, kv] = jnp.concatenate(rest, axis=0).astype(jnp.bfloat16)


def gathered(pieces):
    width = 1024
    shape = jax.ShapeDtypeStruct
    return pl.pallas_call(
        gathered_kernel,
        grid=(FEAT // width,),
        in_specs=[cols(width, 5, 4)] * NZ,
        out_specs=[cols(width, N2), cols(width, N2), cols(width, NXH, 2, N3G)],
        out_shape=[
            pltpu.HBM((N2, FEAT), jnp.bfloat16),
            pltpu.HBM((N2, FEAT), jnp.bfloat16),
            shape((NXH, 2, N3G, FEAT), jnp.bfloat16),
        ],
        compiler_params=pltpu.CompilerParams(vmem_limit_bytes=32 * 1024 * 1024),
        cost_estimate=pl.CostEstimate(flops=1 << 20, bytes_accessed=1 << 20, transcendentals=0),
    )(*pieces)


def lifted_kernel(g2_ref, third_ref, *outs):
    for kv in range(2):
        for s in range(NZ):
            for i in range(NXL):
                row = slice(s * NXL + i, s * NXL + i + 1)
                lift = third_ref[0, kv, row, :] * 0.5
                part = g2_ref[s, kv, i * 4 : i * 4 + 4, :] + lift
                outs[s][kv * NXL + i] = part.astype(outs[s].dtype)
                rest = third_ref[1, kv, row, :]
                outs[s][4, kv * NXL + i : kv * NXL + i + 1, :] = rest.astype(outs[s].dtype)


def lifted(g2, third):
    width = 1024
    shape = jax.ShapeDtypeStruct
    return pl.pallas_call(
        lifted_kernel,
        grid=(FEAT // width,),
        in_specs=[cols(width, NZ, 2, 8), cols(width, NXH, 2, N3G)],
        out_specs=[cols(width, 5, 4)] * NZ,
        out_shape=[
            shape((5, 4, FEAT), jnp.float32 if s == 0 else jnp.bfloat16) for s in range(NZ)
        ],
        compiler_params=pltpu.CompilerParams(vmem_limit_bytes=24 * 1024 * 1024),
        cost_estimate=pl.CostEstimate(flops=1 << 20, bytes_accessed=2 << 20, transcendentals=0),
    )(g2, third)


def finish_kernel(dk_ref, dv_ref, lo_ref, hi_ref, two_ref, gk_ref, gv_ref):
    low = pl.program_id(0) < pl.num_programs(0) // 2
    for kv, src, dst in ((0, dk_ref, gk_ref), (1, dv_ref, gv_ref)):
        for part in range(4):
            lo = part * P2
            spread = two_ref[kv, part : part + 1, :]
            val = src[lo : lo + P2, :].astype(jnp.float32) + spread
            if part >= 2:
                rows = slice(lo - BLK, lo - BLK + P2)
                back = jnp.where(low, lo_ref[kv, rows, :], hi_ref[kv, rows, :])
                val = val + back.astype(jnp.float32)
            dst[lo : lo + P2, :] = val.astype(jnp.bfloat16)


def finish(dk, dv, back_lo, back_hi, two):
    rows = dk.shape[0]
    width = 512
    half = FEAT // width // 2
    shape = jax.ShapeDtypeStruct
    return pl.pallas_call(
        finish_kernel,
        grid=(FEAT // width,),
        in_specs=[cols(width, rows)] * 2 + [
            pl.BlockSpec((2, BLK, width), lambda i: (0, 0, jnp.minimum(i, half - 1))),
            pl.BlockSpec((2, BLK, width), lambda i: (0, 0, jnp.maximum(i - half, 0))),
            cols(width, 2, 4),
        ],
        out_specs=[cols(width, rows)] * 2,
        out_shape=[shape((rows, FEAT), jnp.bfloat16)] * 2,
        compiler_params=pltpu.CompilerParams(vmem_limit_bytes=48 * 1024 * 1024),
        cost_estimate=pl.CostEstimate(flops=1 << 20, bytes_accessed=7 << 20, transcendentals=0),
    )(dk, dv, back_lo, back_hi, two)


def in_hbm(*values):
    return [pltpu.with_memory_space_constraint(v, pltpu.HBM) for v in values]


def ring(value, axis, size, step):
    return lax.ppermute(value, axis, [(i, (i + step) % size) for i in range(size)])


def bf(x):
    return x.astype(jnp.bfloat16)


def f32(x):
    return x.astype(jnp.float32)


def per_device(queries, keys, values, grad_out):
    xh, y, c, z, xl = (lax.axis_index(a) for a in AXES)

    pooled, own = pool(keys, values)
    other = ring(pooled, "xl", NXL, 1)
    near_own = ring(own, "xh", NXH, 1)
    far_own = lax.ppermute(own, ("xh", "xl"), DIAGONAL)
    pair = joined(pooled, other, near_own, far_own)
    pieces = [pair] + [ring(pair, "z", NZ, s) for s in Z_ORDER[::-1]]
    pk2, pv2, third = gathered(pieces)
    mid = FEAT // 2
    lasts = [
        jnp.stack([keys[BLK:, lo : lo + mid], values[BLK:, lo : lo + mid]]) for lo in (0, mid)
    ]
    *lasts, third = lax.optimization_barrier((*lasts, third))
    count = NXH * NY * NC * NZ * NXL
    priors = [lax.ppermute(x, AXES, [(i, i + 1) for i in range(count - 1)]) for x in lasts]
    thirds = [third] + [ring(third, "y", NY, s) for s in Y_STEP[1:]]
    thirds = thirds + [ring(t, "c", NC, 1) for t in thirds]

    place = jnp.stack([xh, y, c, z, xl]).astype(jnp.int32)

    fixed = in_hbm(queries, keys, values, grad_out)
    pools = (*in_hbm(pk2, pv2), in_hbm(*thirds))
    outs, backs = [], []
    for half in range(2):
        *outs, dprior = attention(half, place, *fixed, priors[half], *pools, outs)
        backs.append(lax.ppermute(dprior, AXES, [(i + 1, i) for i in range(count - 1)]))
    attended, grad_q, dk, dv, g2, near, far = outs

    backs[0], far = lax.optimization_barrier((backs[0], far))
    far = ring(far, "c", NC, 1)
    s3 = [f32(near[s]) + f32(far[s]) for s in range(NY)]
    t3 = s3[0]
    for s in (3, 1, 2):
        t3 = t3 + f32(ring(bf(s3[s]), "y", NY, -Y_STEP[s]))
    *backs, t3 = lax.optimization_barrier((*backs, t3))
    parts = lifted(g2, t3)
    two = parts[0]
    for s in Z_ORDER:
        two = two + f32(ring(parts[s], "z", NZ, -s))
    near_third = ring(bf(two[4, 0::2]), "xh", NXH, 1)
    far_third = lax.ppermute(
        bf(two[4, 1::2]), ("xh", "xl"), DIAGONAL
    )
    two = two[0:4:2] + f32(ring(bf(two[1:4:2]), "xl", NXL, 1))
    two = two + 0.5 * (f32(near_third) + f32(far_third))[:, None, :]
    two = two / math.sqrt(P2)
    grad_k, grad_v = finish(dk, dv, *backs, two)
    return attended, grad_q, grad_k, grad_v


def solution(mesh):
    fine_mesh = Mesh(np.asarray(mesh.devices).reshape(NXH, NY, NC, NZ, NXL), AXES)
    spec = P(AXES, None)
    return jax.shard_map(
        per_device,
        mesh=fine_mesh,
        in_specs=(spec,) * 4,
        out_specs=(spec,) * 4,
        check_vma=False,
    )
```

```python
import math

import jax
import jax.numpy as jnp
import numpy as np
from jax import lax
from jax.experimental import pallas as pl
from jax.experimental.pallas import tpu as pltpu
from jax.sharding import Mesh, PartitionSpec as P

HEADS = 16
HDIM = 128
BLK = 128
P2 = 64
FEAT = HEADS * HDIM
NEG_BIG = -1e30
LOG2E = math.log2(math.e)
SCALE = 1.0 / math.sqrt(HDIM)

NXH, NY, NC, NZ, NXL = 2, 4, 2, 8, 2
AXES = ("xh", "y", "c", "z", "xl")
N2 = NZ * NXL * 4
N3G = NZ * NXL
N3 = N3G * NXH * NY * NC
NP = N2 + N3
HPB = 4
Z_ORDER = (4, 5, 3, 6, 2, 7, 1)
Y_STEP = (0, 1, 3, 2)
DIAGONAL = ((0, 3), (1, 2), (2, 1), (3, 0))


def nt(a, b):
    return lax.dot_general(a, b, (((1,), (1,)), ((), ())), preferred_element_type=jnp.float32)


def nn(a, b):
    return lax.dot_general(a, b, (((1,), (0,)), ((), ())), preferred_element_type=jnp.float32)


def tn(a, b):
    return lax.dot_general(a, b, (((0,), (0,)), ((), ())), preferred_element_type=jnp.float32)


def one_head(bias_ref, seg, refs, outs):
    q_ref, k_ref, v_ref, g_ref, prior_ref, pk2_ref, pv2_ref = refs[:7]
    thirds = refs[7:]
    att_ref, dq_ref, dk_ref, dv_ref, g2_ref, near_ref, far_a_ref, far_b_ref, dprior_ref = outs
    q = q_ref[:, seg]
    k = k_ref[:, seg]
    v = v_ref[:, seg]
    g = g_ref[:, seg]
    prior_k = prior_ref[0, :, seg]
    prior_v = prior_ref[1, :, seg]
    pk = jnp.concatenate(
        [pk2_ref[:, seg]] + [t[s, 0, :, seg] for t in thirds for s in range(NXH)], axis=0
    )
    pv = jnp.concatenate(
        [pv2_ref[:, seg]] + [t[s, 1, :, seg] for t in thirds for s in range(NXH)], axis=0
    )
    c2 = SCALE * LOG2E
    key_i = lax.broadcasted_iota(jnp.int32, (BLK, BLK), 0)
    qry_i = lax.broadcasted_iota(jnp.int32, (BLK, BLK), 1)
    causal = key_i <= qry_i
    q0, q1 = q[:BLK], q[BLK:]
    g0, g1 = g[:BLK], g[BLK:]
    k0, k1 = k[:BLK], k[BLK:]
    v0, v1 = v[:BLK], v[BLK:]

    sp = nt(pk, q) * c2 + bias_ref[BLK:, :]
    s_prior = nt(prior_k, q0) * c2 + bias_ref[:BLK, :BLK]
    s_k0 = nt(k0, q) * c2
    s00 = jnp.where(causal, s_k0[:, :BLK], NEG_BIG)
    s01 = s_k0[:, BLK:]
    s11 = jnp.where(causal, nt(k1, q1) * c2, NEG_BIG)

    fine = ((s_prior, s00), (s01, s11))
    fine_k = ((prior_v, v0), (v0, v1))
    expo, invs, atts, deltas = [], [], [], []
    for b in range(2):
        cols = slice(b * BLK, (b + 1) * BLK)
        sa, sb = fine[b]
        spb = sp[:, cols]
        top = jnp.maximum(
            jnp.max(spb, axis=0, keepdims=True), jnp.max(jnp.maximum(sa, sb), axis=0, keepdims=True)
        )
        ea = jnp.exp2(sa - top)
        eb = jnp.exp2(sb - top)
        ep = jnp.exp2(spb - top)
        tot = jnp.sum(ea + eb, axis=0, keepdims=True) + jnp.sum(ep, axis=0, keepdims=True)
        inv = 1.0 / tot
        invs.append(inv)
        expo.append((ea, eb, ep))
    ea_all = [e[0].astype(jnp.bfloat16) for e in expo]
    eb_all = [e[1].astype(jnp.bfloat16) for e in expo]
    ep_all = jnp.concatenate([e[2].astype(jnp.bfloat16) for e in expo], axis=1)
    mixed = tn(pv, ep_all) + tn(v0, jnp.concatenate([eb_all[0], ea_all[1]], axis=1))
    edge = jnp.concatenate([tn(prior_v, ea_all[0]), tn(v1, eb_all[1])], axis=1)
    inv_all = jnp.concatenate(invs, axis=1)
    att_t = ((mixed + edge) * inv_all).astype(jnp.bfloat16)
    att_ref[:, seg] = jnp.transpose(att_t)
    g_t = jnp.transpose(g).astype(jnp.float32)
    delta_all = jnp.sum(g_t * att_t.astype(jnp.float32), axis=0, keepdims=True)
    deltas = [delta_all[:, :BLK], delta_all[:, BLK:]]

    dp = nt(pv, g)
    d_prior = nt(prior_v, g0)
    d_k0 = nt(v0, g)
    d11 = nt(v1, g1)
    dots = ((d_prior, d_k0[:, :BLK]), (d_k0[:, BLK:], d11))
    ws, ds = [], []
    for b in range(2):
        cols = slice(b * BLK, (b + 1) * BLK)
        wts = [e * invs[b] for e in expo[b]]
        dot_b = dots[b] + (dp[:, cols],)
        ws.append([w.astype(jnp.bfloat16) for w in wts])
        ds.append(
            [(w * SCALE * (d - deltas[b])).astype(jnp.bfloat16) for w, d in zip(wts, dot_b)]
        )
    wp = jnp.concatenate([ws[0][2], ws[1][2]], axis=1)
    dsp = jnp.concatenate([ds[0][2], ds[1][2]], axis=1)
    wk0 = jnp.concatenate([ws[0][1], ws[1][0]], axis=1)
    dsk0 = jnp.concatenate([ds[0][1], ds[1][0]], axis=1)

    dq_t = tn(pk, dsp) + tn(k0, dsk0)
    dq_t = dq_t + jnp.concatenate([tn(prior_k, ds[0][0]), tn(k1, ds[1][1])], axis=1)
    dq_ref[:, seg] = jnp.transpose(dq_t.astype(jnp.bfloat16))

    dprior_ref[0, :, seg] = nn(ds[0][0], q0).astype(jnp.bfloat16)
    dprior_ref[1, :, seg] = nn(ws[0][0], g0).astype(jnp.bfloat16)
    dk_ref[:BLK, seg] = nn(dsk0, q).astype(jnp.bfloat16)
    dk_ref[BLK:, seg] = nn(ds[1][1], q1).astype(jnp.bfloat16)
    dv_ref[:BLK, seg] = nn(wk0, g).astype(jnp.bfloat16)
    dv_ref[BLK:, seg] = nn(ws[1][1], g1).astype(jnp.bfloat16)
    gkp = nn(dsp, q)
    gvp = nn(wp, g)
    for kv, part in enumerate((gkp, gvp)):
        for s in range(NZ):
            g2_ref[s, kv, :, seg] = part[s * 8 : s * 8 + 8]
        for s in range(2 * NY * NXH):
            lo = N2 + s * N3G
            slot, value = s // NXH % NY, part[lo : lo + N3G].astype(jnp.bfloat16)
            if s < NY * NXH:
                near_ref[slot, s % NXH, kv, :, seg] = value
            else:
                ref = (far_a_ref, far_b_ref)[slot // 2]
                ref[slot % 2, s % NXH, kv, :, seg] = value


def fill_bias(place_ref, bias_ref):
    xh, y, c, z, xl = (place_ref[i] for i in range(5))
    group = xh * (NY * NC) + y * NC + c
    shard = z * NXL + xl
    first = (group * (NZ * NXL) + shard) == 0
    bias_ref[:BLK, :] = jnp.full((BLK, 2 * BLK), jnp.where(first, NEG_BIG, 0.0), jnp.float32)
    r2 = lax.broadcasted_iota(jnp.int32, (N2, 2 * BLK), 0)
    late = lax.broadcasted_iota(jnp.int32, (N2, 2 * BLK), 1) // BLK
    from_shard = ((z + NZ - r2 // 8) % NZ) * NXL + (xl + r2 // 4) % NXL
    ok2 = from_shard * 4 + r2 % 4 < 4 * shard - 2 + 2 * late
    bias_ref[BLK : BLK + N2, :] = jnp.where(ok2, 0.0, NEG_BIG)
    for s in range(2 * NY * NXH):
        of_xh = (xh + s % NXH) % NXH
        of_y = (y + NY - Y_STEP[s // NXH % NY]) % NY
        of_c = (c + s // (NXH * NY)) % NC
        ok3 = of_xh * (NY * NC) + of_y * NC + of_c < group
        lo = BLK + N2 + s * N3G
        bias_ref[lo : lo + N3G, :] = jnp.full(
            (N3G, 2 * BLK), jnp.where(ok3, 0.0, NEG_BIG), jnp.float32
        )


def attn_kernel(place_ref, *refs):
    bias_ref = refs[-1]

    @pl.when(pl.program_id(0) == 0)
    def _():
        fill_bias(place_ref, bias_ref)

    for h in range(HPB):
        seg = slice(h * HDIM, (h + 1) * HDIM)
        one_head(bias_ref, seg, refs[:15], refs[-10:-1])


def cols(width, *lead, at=0):
    zeros = (0,) * len(lead)
    return pl.BlockSpec(lead + (width,), lambda i: zeros + (i + at,))


def attention(half, place, q, k, v, g, prior, pk2, pv2, thirds, earlier):
    width = HPB * HDIM
    rows = q.shape[0]
    steps = FEAT // width // 2
    at = half * steps
    shape = jax.ShapeDtypeStruct
    row_spec = cols(width, rows, at=at)
    sums_spec = cols(width, NY, NXH, 2, N3G, at=at)
    half_spec = cols(width, NY // 2, NXH, 2, N3G, at=at)
    prior_spec = cols(width, 2, BLK)
    first_alias = 8 + len(thirds)
    return pl.pallas_call(
        attn_kernel,
        grid=(steps,),
        in_specs=[
            pl.BlockSpec(memory_space=pltpu.SMEM),
            row_spec, row_spec, row_spec, row_spec,
            prior_spec, cols(width, N2, at=at), cols(width, N2, at=at),
        ]
        + [cols(width, NXH, 2, N3G, at=at)] * len(thirds)
        + [pl.BlockSpec(memory_space=pl.ANY)] * len(earlier),
        out_specs=[
            row_spec, row_spec, row_spec, row_spec,
            cols(width, NZ, 2, 8, at=at), sums_spec, half_spec, half_spec, prior_spec,
        ],
        out_shape=[
            shape((rows, FEAT), jnp.bfloat16),
            shape((rows, FEAT), jnp.bfloat16),
            shape((rows, FEAT), jnp.bfloat16),
            shape((rows, FEAT), jnp.bfloat16),
            shape((NZ, 2, 8, FEAT), jnp.float32),
            shape((NY, NXH, 2, N3G, FEAT), jnp.bfloat16),
            shape((NY // 2, NXH, 2, N3G, FEAT), jnp.bfloat16),
            shape((NY // 2, NXH, 2, N3G, FEAT), jnp.bfloat16),
            shape((2, BLK, FEAT // 2), jnp.bfloat16),
        ],
        scratch_shapes=[pltpu.VMEM((BLK + NP, 2 * BLK), jnp.float32)],
        input_output_aliases={first_alias + i: i for i in range(len(earlier))},
        compiler_params=pltpu.CompilerParams(vmem_limit_bytes=24 * 1024 * 1024),
        cost_estimate=pl.CostEstimate(
            flops=6 * 2 * BLK * 576 * FEAT, bytes_accessed=10 << 20, transcendentals=0
        ),
    )(place, q, k, v, g, prior, pk2, pv2, *thirds, *earlier)


def pool(k, v):
    runs = jnp.stack([k, v]).astype(jnp.float32).reshape(2, 4, P2, FEAT)
    pooled = (jnp.sum(runs, axis=2) / math.sqrt(P2)).astype(jnp.bfloat16)
    third = jnp.sum(pooled.astype(jnp.float32), axis=1) * 0.5
    return pooled, third.astype(jnp.bfloat16)


def joined_kernel(mine_ref, other_ref, near_ref, far_ref, out_ref):
    for kv in range(2):
        out_ref[kv * NXL] = mine_ref[kv]
        out_ref[kv * NXL + 1] = other_ref[kv]
        out_ref[4, kv * NXL : kv * NXL + 1, :] = near_ref[kv : kv + 1, :]
        out_ref[4, kv * NXL + 1 : kv * NXL + 2, :] = far_ref[kv : kv + 1, :]


def joined(mine, other, near, far):
    width = FEAT
    return pl.pallas_call(
        joined_kernel,
        grid=(1,),
        in_specs=[cols(width, 2, 4), cols(width, 2, 4), cols(width, 2), cols(width, 2)],
        out_specs=cols(width, 5, 4),
        out_shape=jax.ShapeDtypeStruct((5, 4, FEAT), jnp.bfloat16),
        compiler_params=pltpu.CompilerParams(vmem_limit_bytes=24 * 1024 * 1024),
        cost_estimate=pl.CostEstimate(flops=1 << 10, bytes_accessed=1 << 18, transcendentals=0),
    )(mine, other, near, far)


def gathered_kernel(*refs):
    by_step = dict(zip((0,) + Z_ORDER[::-1], refs[:NZ]))
    pieces, (pk_ref, pv_ref, third_ref) = [by_step[s] for s in range(NZ)], refs[NZ:]
    for kv, out in ((0, pk_ref), (1, pv_ref)):
        runs = [p[kv * NXL + i].astype(jnp.float32) for p in pieces for i in range(NXL)]
        out[...] = jnp.concatenate(runs, axis=0).astype(jnp.bfloat16)
        sums = [jnp.sum(r, axis=0, keepdims=True) * 0.5 for r in runs]
        third_ref[0, kv] = jnp.concatenate(sums, axis=0).astype(jnp.bfloat16)
        rest = [p[4, kv * NXL : kv * NXL + NXL, :].astype(jnp.float32) for p in pieces]
        third_ref[1, kv] = jnp.concatenate(rest, axis=0).astype(jnp.bfloat16)


def gathered(pieces):
    width = 1024
    shape = jax.ShapeDtypeStruct
    return pl.pallas_call(
        gathered_kernel,
        grid=(FEAT // width,),
        in_specs=[cols(width, 5, 4)] * NZ,
        out_specs=[cols(width, N2), cols(width, N2), cols(width, NXH, 2, N3G)],
        out_shape=[
            pltpu.HBM((N2, FEAT), jnp.bfloat16),
            pltpu.HBM((N2, FEAT), jnp.bfloat16),
            shape((NXH, 2, N3G, FEAT), jnp.bfloat16),
        ],
        compiler_params=pltpu.CompilerParams(vmem_limit_bytes=32 * 1024 * 1024),
        cost_estimate=pl.CostEstimate(flops=1 << 20, bytes_accessed=1 << 20, transcendentals=0),
    )(*pieces)


def lifted_kernel(g2_ref, third_ref, *outs):
    for kv in range(2):
        for s in range(NZ):
            for i in range(NXL):
                row = slice(s * NXL + i, s * NXL + i + 1)
                lift = third_ref[0, kv, row, :] * 0.5
                part = g2_ref[s, kv, i * 4 : i * 4 + 4, :] + lift
                outs[s][kv * NXL + i] = part.astype(outs[s].dtype)
                rest = third_ref[1, kv, row, :]
                outs[s][4, kv * NXL + i : kv * NXL + i + 1, :] = rest.astype(outs[s].dtype)


def lifted(g2, third):
    width = 1024
    shape = jax.ShapeDtypeStruct
    return pl.pallas_call(
        lifted_kernel,
        grid=(FEAT // width,),
        in_specs=[cols(width, NZ, 2, 8), cols(width, NXH, 2, N3G)],
        out_specs=[cols(width, 5, 4)] * NZ,
        out_shape=[
            shape((5, 4, FEAT), jnp.float32 if s == 0 else jnp.bfloat16) for s in range(NZ)
        ],
        compiler_params=pltpu.CompilerParams(vmem_limit_bytes=24 * 1024 * 1024),
        cost_estimate=pl.CostEstimate(flops=1 << 20, bytes_accessed=2 << 20, transcendentals=0),
    )(g2, third)


def finish_kernel(dk_ref, dv_ref, lo_ref, hi_ref, two_ref, gk_ref, gv_ref):
    low = pl.program_id(0) < pl.num_programs(0) // 2
    for kv, src, dst in ((0, dk_ref, gk_ref), (1, dv_ref, gv_ref)):
        for part in range(4):
            lo = part * P2
            spread = two_ref[kv, part : part + 1, :]
            val = src[lo : lo + P2, :].astype(jnp.float32) + spread
            if part >= 2:
                rows = slice(lo - BLK, lo - BLK + P2)
                back = jnp.where(low, lo_ref[kv, rows, :], hi_ref[kv, rows, :])
                val = val + back.astype(jnp.float32)
            dst[lo : lo + P2, :] = val.astype(jnp.bfloat16)


def finish(dk, dv, back_lo, back_hi, two):
    rows = dk.shape[0]
    width = 512
    half = FEAT // width // 2
    shape = jax.ShapeDtypeStruct
    return pl.pallas_call(
        finish_kernel,
        grid=(FEAT // width,),
        in_specs=[cols(width, rows)] * 2 + [
            pl.BlockSpec((2, BLK, width), lambda i: (0, 0, jnp.minimum(i, half - 1))),
            pl.BlockSpec((2, BLK, width), lambda i: (0, 0, jnp.maximum(i - half, 0))),
            cols(width, 2, 4),
        ],
        out_specs=[cols(width, rows)] * 2,
        out_shape=[shape((rows, FEAT), jnp.bfloat16)] * 2,
        compiler_params=pltpu.CompilerParams(vmem_limit_bytes=48 * 1024 * 1024),
        cost_estimate=pl.CostEstimate(flops=1 << 20, bytes_accessed=7 << 20, transcendentals=0),
    )(dk, dv, back_lo, back_hi, two)


def in_hbm(*values):
    return [pltpu.with_memory_space_constraint(v, pltpu.HBM) for v in values]


def ring(value, axis, size, step):
    return lax.ppermute(value, axis, [(i, (i + step) % size) for i in range(size)])


def bf(x):
    return x.astype(jnp.bfloat16)


def f32(x):
    return x.astype(jnp.float32)


def per_device(queries, keys, values, grad_out):
    xh, y, c, z, xl = (lax.axis_index(a) for a in AXES)

    pooled, own = pool(keys, values)
    other = ring(pooled, "xl", NXL, 1)
    near_own = ring(own, "xh", NXH, 1)
    far_own = lax.ppermute(own, ("xh", "xl"), DIAGONAL)
    pair = joined(pooled, other, near_own, far_own)
    pieces = [pair] + [ring(pair, "z", NZ, s) for s in Z_ORDER[::-1]]
    pk2, pv2, third = gathered(pieces)
    mid = FEAT // 2
    lasts = [
        jnp.stack([keys[BLK:, lo : lo + mid], values[BLK:, lo : lo + mid]]) for lo in (0, mid)
    ]
    *lasts, third = lax.optimization_barrier((*lasts, third))
    count = NXH * NY * NC * NZ * NXL
    priors = [lax.ppermute(x, AXES, [(i, i + 1) for i in range(count - 1)]) for x in lasts]
    thirds = [third] + [ring(third, "y", NY, s) for s in Y_STEP[1:]]
    thirds = thirds + [ring(t, "c", NC, 1) for t in thirds]

    place = jnp.stack([xh, y, c, z, xl]).astype(jnp.int32)

    fixed = in_hbm(queries, keys, values, grad_out)
    pools = (*in_hbm(pk2, pv2), in_hbm(*thirds))
    outs, backs = [], []
    for half in range(2):
        *outs, dprior = attention(half, place, *fixed, priors[half], *pools, outs)
        backs.append(lax.ppermute(dprior, AXES, [(i + 1, i) for i in range(count - 1)]))
    attended, grad_q, dk, dv, g2, near, far_a, far_b = outs

    backs[0], far_a = lax.optimization_barrier((backs[0], far_a))
    far_a, far_b = ring(far_a, "c", NC, 1), ring(far_b, "c", NC, 1)
    far = [far_a[0], far_a[1], far_b[0], far_b[1]]
    s3 = [f32(near[s]) + f32(far[s]) for s in range(NY)]
    t3 = s3[0]
    for s in (3, 1, 2):
        t3 = t3 + f32(ring(bf(s3[s]), "y", NY, -Y_STEP[s]))
    *backs, t3 = lax.optimization_barrier((*backs, t3))
    parts = lifted(g2, t3)
    two = parts[0]
    for s in Z_ORDER:
        two = two + f32(ring(parts[s], "z", NZ, -s))
    near_third = ring(bf(two[4, 0::2]), "xh", NXH, 1)
    far_third = lax.ppermute(
        bf(two[4, 1::2]), ("xh", "xl"), DIAGONAL
    )
    two = two[0:4:2] + f32(ring(bf(two[1:4:2]), "xl", NXL, 1))
    two = two + 0.5 * (f32(near_third) + f32(far_third))[:, None, :]
    two = two / math.sqrt(P2)
    grad_k, grad_v = finish(dk, dv, *backs, two)
    return attended, grad_q, grad_k, grad_v


def solution(mesh):
    fine_mesh = Mesh(np.asarray(mesh.devices).reshape(NXH, NY, NC, NZ, NXL), AXES)
    spec = P(AXES, None)
    return jax.shard_map(
        per_device,
        mesh=fine_mesh,
        in_specs=(spec,) * 4,
        out_specs=(spec,) * 4,
        check_vma=False,
    )
```

```python
import math

import jax
import jax.numpy as jnp
import numpy as np
from jax import lax
from jax.experimental import pallas as pl
from jax.experimental.pallas import tpu as pltpu
from jax.sharding import Mesh, PartitionSpec as P

HEADS = 16
HDIM = 128
BLK = 128
P2 = 64
FEAT = HEADS * HDIM
NEG_BIG = -1e30
LOG2E = math.log2(math.e)
SCALE = 1.0 / math.sqrt(HDIM)

NXH, NY, NC, NZ, NXL = 2, 4, 2, 8, 2
AXES = ("xh", "y", "c", "z", "xl")
N2 = NZ * NXL * 4
N3G = NZ * NXL
N3 = N3G * NXH * NY * NC
NP = N2 + N3
HPB = 4
Z_ORDER = (3, 5, 4, 2, 6, 1, 7)
Y_STEP = (0, 1, 3, 2)
DIAGONAL = ((0, 3), (1, 2), (2, 1), (3, 0))


def nt(a, b):
    return lax.dot_general(a, b, (((1,), (1,)), ((), ())), preferred_element_type=jnp.float32)


def nn(a, b):
    return lax.dot_general(a, b, (((1,), (0,)), ((), ())), preferred_element_type=jnp.float32)


def tn(a, b):
    return lax.dot_general(a, b, (((0,), (0,)), ((), ())), preferred_element_type=jnp.float32)


def one_head(bias_ref, seg, refs, outs):
    q_ref, k_ref, v_ref, g_ref, prior_ref, pk2_ref, pv2_ref = refs[:7]
    thirds = refs[7:]
    att_ref, dq_ref, dk_ref, dv_ref, g2_ref, near_ref, far_a_ref, far_b_ref, dprior_ref = outs
    q = q_ref[:, seg]
    k = k_ref[:, seg]
    v = v_ref[:, seg]
    g = g_ref[:, seg]
    prior_k = prior_ref[0, :, seg]
    prior_v = prior_ref[1, :, seg]
    pk = jnp.concatenate(
        [pk2_ref[:, seg]] + [t[s, 0, :, seg] for t in thirds for s in range(NXH)], axis=0
    )
    pv = jnp.concatenate(
        [pv2_ref[:, seg]] + [t[s, 1, :, seg] for t in thirds for s in range(NXH)], axis=0
    )
    c2 = SCALE * LOG2E
    key_i = lax.broadcasted_iota(jnp.int32, (BLK, BLK), 0)
    qry_i = lax.broadcasted_iota(jnp.int32, (BLK, BLK), 1)
    causal = key_i <= qry_i
    q0, q1 = q[:BLK], q[BLK:]
    g0, g1 = g[:BLK], g[BLK:]
    k0, k1 = k[:BLK], k[BLK:]
    v0, v1 = v[:BLK], v[BLK:]

    sp = nt(pk, q) * c2 + bias_ref[BLK:, :]
    s_prior = nt(prior_k, q0) * c2 + bias_ref[:BLK, :BLK]
    s_k0 = nt(k0, q) * c2
    s00 = jnp.where(causal, s_k0[:, :BLK], NEG_BIG)
    s01 = s_k0[:, BLK:]
    s11 = jnp.where(causal, nt(k1, q1) * c2, NEG_BIG)

    fine = ((s_prior, s00), (s01, s11))
    fine_k = ((prior_v, v0), (v0, v1))
    expo, invs, atts, deltas = [], [], [], []
    for b in range(2):
        cols = slice(b * BLK, (b + 1) * BLK)
        sa, sb = fine[b]
        spb = sp[:, cols]
        top = jnp.maximum(
            jnp.max(spb, axis=0, keepdims=True), jnp.max(jnp.maximum(sa, sb), axis=0, keepdims=True)
        )
        ea = jnp.exp2(sa - top)
        eb = jnp.exp2(sb - top)
        ep = jnp.exp2(spb - top)
        tot = jnp.sum(ea + eb, axis=0, keepdims=True) + jnp.sum(ep, axis=0, keepdims=True)
        inv = 1.0 / tot
        invs.append(inv)
        expo.append((ea, eb, ep))
    ea_all = [e[0].astype(jnp.bfloat16) for e in expo]
    eb_all = [e[1].astype(jnp.bfloat16) for e in expo]
    ep_all = jnp.concatenate([e[2].astype(jnp.bfloat16) for e in expo], axis=1)
    mixed = tn(pv, ep_all) + tn(v0, jnp.concatenate([eb_all[0], ea_all[1]], axis=1))
    edge = jnp.concatenate([tn(prior_v, ea_all[0]), tn(v1, eb_all[1])], axis=1)
    inv_all = jnp.concatenate(invs, axis=1)
    att_t = ((mixed + edge) * inv_all).astype(jnp.bfloat16)
    att_ref[:, seg] = jnp.transpose(att_t)
    g_t = jnp.transpose(g).astype(jnp.float32)
    delta_all = jnp.sum(g_t * att_t.astype(jnp.float32), axis=0, keepdims=True)
    deltas = [delta_all[:, :BLK], delta_all[:, BLK:]]

    dp = nt(pv, g)
    d_prior = nt(prior_v, g0)
    d_k0 = nt(v0, g)
    d11 = nt(v1, g1)
    dots = ((d_prior, d_k0[:, :BLK]), (d_k0[:, BLK:], d11))
    ws, ds = [], []
    for b in range(2):
        cols = slice(b * BLK, (b + 1) * BLK)
        wts = [e * invs[b] for e in expo[b]]
        dot_b = dots[b] + (dp[:, cols],)
        ws.append([w.astype(jnp.bfloat16) for w in wts])
        ds.append(
            [(w * SCALE * (d - deltas[b])).astype(jnp.bfloat16) for w, d in zip(wts, dot_b)]
        )
    wp = jnp.concatenate([ws[0][2], ws[1][2]], axis=1)
    dsp = jnp.concatenate([ds[0][2], ds[1][2]], axis=1)
    wk0 = jnp.concatenate([ws[0][1], ws[1][0]], axis=1)
    dsk0 = jnp.concatenate([ds[0][1], ds[1][0]], axis=1)

    dq_t = tn(pk, dsp) + tn(k0, dsk0)
    dq_t = dq_t + jnp.concatenate([tn(prior_k, ds[0][0]), tn(k1, ds[1][1])], axis=1)
    dq_ref[:, seg] = jnp.transpose(dq_t.astype(jnp.bfloat16))

    dprior_ref[0, :, seg] = nn(ds[0][0], q0).astype(jnp.bfloat16)
    dprior_ref[1, :, seg] = nn(ws[0][0], g0).astype(jnp.bfloat16)
    dk_ref[:BLK, seg] = nn(dsk0, q).astype(jnp.bfloat16)
    dk_ref[BLK:, seg] = nn(ds[1][1], q1).astype(jnp.bfloat16)
    dv_ref[:BLK, seg] = nn(wk0, g).astype(jnp.bfloat16)
    dv_ref[BLK:, seg] = nn(ws[1][1], g1).astype(jnp.bfloat16)
    gkp = nn(dsp, q)
    gvp = nn(wp, g)
    for kv, part in enumerate((gkp, gvp)):
        for s in range(NZ):
            g2_ref[s, kv, :, seg] = part[s * 8 : s * 8 + 8]
        for s in range(2 * NY * NXH):
            lo = N2 + s * N3G
            slot, value = s // NXH % NY, part[lo : lo + N3G].astype(jnp.bfloat16)
            if s < NY * NXH:
                near_ref[slot, s % NXH, kv, :, seg] = value
            else:
                ref = (far_a_ref, far_b_ref)[slot // 2]
                ref[slot % 2, s % NXH, kv, :, seg] = value


def fill_bias(place_ref, bias_ref):
    xh, y, c, z, xl = (place_ref[i] for i in range(5))
    group = xh * (NY * NC) + y * NC + c
    shard = z * NXL + xl
    first = (group * (NZ * NXL) + shard) == 0
    bias_ref[:BLK, :] = jnp.full((BLK, 2 * BLK), jnp.where(first, NEG_BIG, 0.0), jnp.float32)
    r2 = lax.broadcasted_iota(jnp.int32, (N2, 2 * BLK), 0)
    late = lax.broadcasted_iota(jnp.int32, (N2, 2 * BLK), 1) // BLK
    from_shard = ((z + NZ - r2 // 8) % NZ) * NXL + (xl + r2 // 4) % NXL
    ok2 = from_shard * 4 + r2 % 4 < 4 * shard - 2 + 2 * late
    bias_ref[BLK : BLK + N2, :] = jnp.where(ok2, 0.0, NEG_BIG)
    for s in range(2 * NY * NXH):
        of_xh = (xh + s % NXH) % NXH
        of_y = (y + NY - Y_STEP[s // NXH % NY]) % NY
        of_c = (c + s // (NXH * NY)) % NC
        ok3 = of_xh * (NY * NC) + of_y * NC + of_c < group
        lo = BLK + N2 + s * N3G
        bias_ref[lo : lo + N3G, :] = jnp.full(
            (N3G, 2 * BLK), jnp.where(ok3, 0.0, NEG_BIG), jnp.float32
        )


def attn_kernel(place_ref, *refs):
    bias_ref = refs[-1]

    @pl.when(pl.program_id(0) == 0)
    def _():
        fill_bias(place_ref, bias_ref)

    for h in range(HPB):
        seg = slice(h * HDIM, (h + 1) * HDIM)
        one_head(bias_ref, seg, refs[:15], refs[-10:-1])


def cols(width, *lead, at=0):
    zeros = (0,) * len(lead)
    return pl.BlockSpec(lead + (width,), lambda i: zeros + (i + at,))


def attention(half, place, q, k, v, g, prior, pk2, pv2, thirds, earlier):
    width = HPB * HDIM
    rows = q.shape[0]
    steps = FEAT // width // 2
    at = half * steps
    shape = jax.ShapeDtypeStruct
    row_spec = cols(width, rows, at=at)
    sums_spec = cols(width, NY, NXH, 2, N3G, at=at)
    half_spec = cols(width, NY // 2, NXH, 2, N3G, at=at)
    prior_spec = cols(width, 2, BLK)
    first_alias = 8 + len(thirds)
    return pl.pallas_call(
        attn_kernel,
        grid=(steps,),
        in_specs=[
            pl.BlockSpec(memory_space=pltpu.SMEM),
            row_spec, row_spec, row_spec, row_spec,
            prior_spec, cols(width, N2, at=at), cols(width, N2, at=at),
        ]
        + [cols(width, NXH, 2, N3G, at=at)] * len(thirds)
        + [pl.BlockSpec(memory_space=pl.ANY)] * len(earlier),
        out_specs=[
            row_spec, row_spec, row_spec, row_spec,
            cols(width, NZ, 2, 8, at=at), sums_spec, half_spec, half_spec, prior_spec,
        ],
        out_shape=[
            shape((rows, FEAT), jnp.bfloat16),
            shape((rows, FEAT), jnp.bfloat16),
            shape((rows, FEAT), jnp.bfloat16),
            shape((rows, FEAT), jnp.bfloat16),
            shape((NZ, 2, 8, FEAT), jnp.float32),
            shape((NY, NXH, 2, N3G, FEAT), jnp.bfloat16),
            shape((NY // 2, NXH, 2, N3G, FEAT), jnp.bfloat16),
            shape((NY // 2, NXH, 2, N3G, FEAT), jnp.bfloat16),
            shape((2, BLK, FEAT // 2), jnp.bfloat16),
        ],
        scratch_shapes=[pltpu.VMEM((BLK + NP, 2 * BLK), jnp.float32)],
        input_output_aliases={first_alias + i: i for i in range(len(earlier))},
        compiler_params=pltpu.CompilerParams(vmem_limit_bytes=24 * 1024 * 1024),
        cost_estimate=pl.CostEstimate(
            flops=6 * 2 * BLK * 576 * FEAT, bytes_accessed=10 << 20, transcendentals=0
        ),
    )(place, q, k, v, g, prior, pk2, pv2, *thirds, *earlier)


def pool(k, v):
    runs = jnp.stack([k, v]).astype(jnp.float32).reshape(2, 4, P2, FEAT)
    pooled = (jnp.sum(runs, axis=2) / math.sqrt(P2)).astype(jnp.bfloat16)
    third = jnp.sum(pooled.astype(jnp.float32), axis=1) * 0.5
    return pooled, third.astype(jnp.bfloat16)


def joined_kernel(mine_ref, other_ref, near_ref, far_ref, out_ref):
    for kv in range(2):
        out_ref[kv * NXL] = mine_ref[kv]
        out_ref[kv * NXL + 1] = other_ref[kv]
        out_ref[4, kv * NXL : kv * NXL + 1, :] = near_ref[kv : kv + 1, :]
        out_ref[4, kv * NXL + 1 : kv * NXL + 2, :] = far_ref[kv : kv + 1, :]


def joined(mine, other, near, far):
    width = FEAT
    return pl.pallas_call(
        joined_kernel,
        grid=(1,),
        in_specs=[cols(width, 2, 4), cols(width, 2, 4), cols(width, 2), cols(width, 2)],
        out_specs=cols(width, 5, 4),
        out_shape=jax.ShapeDtypeStruct((5, 4, FEAT), jnp.bfloat16),
        compiler_params=pltpu.CompilerParams(vmem_limit_bytes=24 * 1024 * 1024),
        cost_estimate=pl.CostEstimate(flops=1 << 10, bytes_accessed=1 << 18, transcendentals=0),
    )(mine, other, near, far)


def gathered_kernel(*refs):
    by_step = dict(zip((0,) + Z_ORDER[::-1], refs[:NZ]))
    pieces, (pk_ref, pv_ref, third_ref) = [by_step[s] for s in range(NZ)], refs[NZ:]
    for kv, out in ((0, pk_ref), (1, pv_ref)):
        runs = [p[kv * NXL + i].astype(jnp.float32) for p in pieces for i in range(NXL)]
        out[...] = jnp.concatenate(runs, axis=0).astype(jnp.bfloat16)
        sums = [jnp.sum(r, axis=0, keepdims=True) * 0.5 for r in runs]
        third_ref[0, kv] = jnp.concatenate(sums, axis=0).astype(jnp.bfloat16)
        rest = [p[4, kv * NXL : kv * NXL + NXL, :].astype(jnp.float32) for p in pieces]
        third_ref[1, kv] = jnp.concatenate(rest, axis=0).astype(jnp.bfloat16)


def gathered(pieces):
    width = 1024
    shape = jax.ShapeDtypeStruct
    return pl.pallas_call(
        gathered_kernel,
        grid=(FEAT // width,),
        in_specs=[cols(width, 5, 4)] * NZ,
        out_specs=[cols(width, N2), cols(width, N2), cols(width, NXH, 2, N3G)],
        out_shape=[
            pltpu.HBM((N2, FEAT), jnp.bfloat16),
            pltpu.HBM((N2, FEAT), jnp.bfloat16),
            shape((NXH, 2, N3G, FEAT), jnp.bfloat16),
        ],
        compiler_params=pltpu.CompilerParams(vmem_limit_bytes=32 * 1024 * 1024),
        cost_estimate=pl.CostEstimate(flops=1 << 20, bytes_accessed=1 << 20, transcendentals=0),
    )(*pieces)


def lifted_kernel(g2_ref, third_ref, *outs):
    for kv in range(2):
        for s in range(NZ):
            for i in range(NXL):
                row = slice(s * NXL + i, s * NXL + i + 1)
                lift = third_ref[0, kv, row, :] * 0.5
                part = g2_ref[s, kv, i * 4 : i * 4 + 4, :] + lift
                outs[s][kv * NXL + i] = part.astype(outs[s].dtype)
                rest = third_ref[1, kv, row, :]
                outs[s][4, kv * NXL + i : kv * NXL + i + 1, :] = rest.astype(outs[s].dtype)


def lifted(g2, third):
    width = 1024
    shape = jax.ShapeDtypeStruct
    return pl.pallas_call(
        lifted_kernel,
        grid=(FEAT // width,),
        in_specs=[cols(width, NZ, 2, 8), cols(width, NXH, 2, N3G)],
        out_specs=[cols(width, 5, 4)] * NZ,
        out_shape=[
            shape((5, 4, FEAT), jnp.float32 if s == 0 else jnp.bfloat16) for s in range(NZ)
        ],
        compiler_params=pltpu.CompilerParams(vmem_limit_bytes=24 * 1024 * 1024),
        cost_estimate=pl.CostEstimate(flops=1 << 20, bytes_accessed=2 << 20, transcendentals=0),
    )(g2, third)


def finish_kernel(dk_ref, dv_ref, lo_ref, hi_ref, two_ref, gk_ref, gv_ref):
    low = pl.program_id(0) < pl.num_programs(0) // 2
    for kv, src, dst in ((0, dk_ref, gk_ref), (1, dv_ref, gv_ref)):
        for part in range(4):
            lo = part * P2
            spread = two_ref[kv, part : part + 1, :]
            val = src[lo : lo + P2, :].astype(jnp.float32) + spread
            if part >= 2:
                rows = slice(lo - BLK, lo - BLK + P2)
                back = jnp.where(low, lo_ref[kv, rows, :], hi_ref[kv, rows, :])
                val = val + back.astype(jnp.float32)
            dst[lo : lo + P2, :] = val.astype(jnp.bfloat16)


def finish(dk, dv, back_lo, back_hi, two):
    rows = dk.shape[0]
    width = 512
    half = FEAT // width // 2
    shape = jax.ShapeDtypeStruct
    return pl.pallas_call(
        finish_kernel,
        grid=(FEAT // width,),
        in_specs=[cols(width, rows)] * 2 + [
            pl.BlockSpec((2, BLK, width), lambda i: (0, 0, jnp.minimum(i, half - 1))),
            pl.BlockSpec((2, BLK, width), lambda i: (0, 0, jnp.maximum(i - half, 0))),
            cols(width, 2, 4),
        ],
        out_specs=[cols(width, rows)] * 2,
        out_shape=[shape((rows, FEAT), jnp.bfloat16)] * 2,
        compiler_params=pltpu.CompilerParams(vmem_limit_bytes=48 * 1024 * 1024),
        cost_estimate=pl.CostEstimate(flops=1 << 20, bytes_accessed=7 << 20, transcendentals=0),
    )(dk, dv, back_lo, back_hi, two)


def in_hbm(*values):
    return [pltpu.with_memory_space_constraint(v, pltpu.HBM) for v in values]


def ring(value, axis, size, step):
    return lax.ppermute(value, axis, [(i, (i + step) % size) for i in range(size)])


def bf(x):
    return x.astype(jnp.bfloat16)


def f32(x):
    return x.astype(jnp.float32)


def per_device(queries, keys, values, grad_out):
    xh, y, c, z, xl = (lax.axis_index(a) for a in AXES)

    pooled, own = pool(keys, values)
    other = ring(pooled, "xl", NXL, 1)
    near_own = ring(own, "xh", NXH, 1)
    far_own = lax.ppermute(own, ("xh", "xl"), DIAGONAL)
    pair = joined(pooled, other, near_own, far_own)
    pieces = [pair] + [ring(pair, "z", NZ, s) for s in Z_ORDER[::-1]]
    pk2, pv2, third = gathered(pieces)
    mid = FEAT // 2
    lasts = [
        jnp.stack([keys[BLK:, lo : lo + mid], values[BLK:, lo : lo + mid]]) for lo in (0, mid)
    ]
    *lasts, third = lax.optimization_barrier((*lasts, third))
    count = NXH * NY * NC * NZ * NXL
    priors = [lax.ppermute(x, AXES, [(i, i + 1) for i in range(count - 1)]) for x in lasts]
    thirds = [third] + [ring(third, "y", NY, s) for s in Y_STEP[1:]]
    thirds = thirds + [ring(t, "c", NC, 1) for t in thirds]

    place = jnp.stack([xh, y, c, z, xl]).astype(jnp.int32)

    fixed = in_hbm(queries, keys, values, grad_out)
    pools = (*in_hbm(pk2, pv2), in_hbm(*thirds))
    outs, backs = [], []
    for half in range(2):
        *outs, dprior = attention(half, place, *fixed, priors[half], *pools, outs)
        backs.append(lax.ppermute(dprior, AXES, [(i + 1, i) for i in range(count - 1)]))
    attended, grad_q, dk, dv, g2, near, far_a, far_b = outs

    backs[0], far_a = lax.optimization_barrier((backs[0], far_a))
    far_a, far_b = ring(far_a, "c", NC, 1), ring(far_b, "c", NC, 1)
    far = [far_a[0], far_a[1], far_b[0], far_b[1]]
    s3 = [f32(near[s]) + f32(far[s]) for s in range(NY)]
    t3 = s3[0]
    for s in (3, 1, 2):
        t3 = t3 + f32(ring(bf(s3[s]), "y", NY, -Y_STEP[s]))
    *backs, t3 = lax.optimization_barrier((*backs, t3))
    parts = lifted(g2, t3)
    two = parts[0]
    for s in Z_ORDER:
        two = two + f32(ring(parts[s], "z", NZ, -s))
    near_third = ring(bf(two[4, 0::2]), "xh", NXH, 1)
    far_third = lax.ppermute(
        bf(two[4, 1::2]), ("xh", "xl"), DIAGONAL
    )
    two = two[0:4:2] + f32(ring(bf(two[1:4:2]), "xl", NXL, 1))
    two = two + 0.5 * (f32(near_third) + f32(far_third))[:, None, :]
    two = two / math.sqrt(P2)
    grad_k, grad_v = finish(dk, dv, *backs, two)
    return attended, grad_q, grad_k, grad_v


def solution(mesh):
    fine_mesh = Mesh(np.asarray(mesh.devices).reshape(NXH, NY, NC, NZ, NXL), AXES)
    spec = P(AXES, None)
    return jax.shard_map(
        per_device,
        mesh=fine_mesh,
        in_specs=(spec,) * 4,
        out_specs=(spec,) * 4,
        check_vma=False,
    )
```
